256 devices in a mesh: row: 4 (over x), vocab: 64 (over y, z, core).
Axes of the slice: x: 4, y: 4, z: 8, core: 2. Of those that a mesh axis runs over, the one named last changes fastest.
Arguments:
- teacher_hidden: bfloat16 [512, 4608], P('vocab', 'row'), may hold values from -35 to 35
- student_hidden: bfloat16 [512, 3584], P('vocab', 'row'), may hold values from -35 to 35
- teacher_weight: bfloat16 [4608, 128000], P('row', 'vocab'), may hold values from -0.1875 to 0.1875
- student_weight: bfloat16 [3584, 128000], P('row', 'vocab'), may hold values from -0.1875 to 0.1875
- sampled_ids: int32 [512], P('row'), may hold values from 0 to 127999
Outputs:
- reverse_kl: float32 [512], P('row')
- chosen_logprob: float32 [2, 512], P(None, 'row')
- logit_grad: bfloat16 [512, 128000], P('row', 'vocab')
- weight_grad: bfloat16 [3584, 128000], P('row', 'vocab')
- hidden_grad: bfloat16 [512, 3584], P('vocab', 'row')
The draws below stay inside these ranges and needn't reach their ends.
All inputs are finite; a program needn't handle non-finite values.
Results may differ from the reference program's by a relative error of at most 0.01.
Values may be sent and summed in bfloat16 or wider, within the bound.
A program may use at most 128 MiB of HBM per device.

```python
import math
import jax
import jax.numpy as jnp

DT = 4608
DS = 3584
TOKENS = 512
VOCAB = 128000


def draw_teacher_hidden(key, part):
    key = jax.random.fold_in(key, 11)
    key_scale, key_base = jax.random.split(key, 2)
    scales = jnp.exp(jax.random.uniform(key_scale, (TOKENS, 1), jnp.float32, math.log(0.7), math.log(7.0)))
    base = jax.random.normal(key_base, (TOKENS, DT), jnp.float32)
    base = jnp.clip(base, -5.0, 5.0)
    return (base * scales).astype(jnp.bfloat16)


def draw_student_hidden(key, part):
    key = jax.random.fold_in(key, 12)
    key_scale, key_base = jax.random.split(key, 2)
    scales = jnp.exp(jax.random.uniform(key_scale, (TOKENS, 1), jnp.float32, math.log(0.7), math.log(7.0)))
    base = jax.random.normal(key_base, (TOKENS, DS), jnp.float32)
    base = jnp.clip(base, -5.0, 5.0)
    return (base * scales).astype(jnp.bfloat16)


def touch_ends(entries, rng, smallest, largest):
    longest = entries.shape.index(max(entries.shape))
    spots = []
    for shift in (0, 1):
        where = [jax.random.randint(jax.random.fold_in(rng, axis), (), 0, length) for axis, length in enumerate(entries.shape)]
        where[longest] = (where[longest] + shift) % entries.shape[longest]
        spots.append(tuple(where))
    return entries.at[spots[0]].set(smallest).at[spots[1]].set(largest)


def block_scale(own_key, shape, shards, smallest, top_value):
    gain, own = 1.0, jax.random.fold_in(own_key, 6)
    for axis_at, shards_of in shards:
        steps = jnp.exp(jax.random.uniform(jax.random.fold_in(own, axis_at), (shards_of,), jnp.float32, smallest / len(shards), top_value / len(shards)))
        gain = gain * jnp.repeat(steps, shape[axis_at] // shards_of).reshape([-1 if axis == axis_at else 1 for axis in range(len(shape))])
    return gain


def normal_values(rng, shape, width, most, shards=(), kind=jnp.bfloat16):
    array = width * jax.random.normal(rng, shape, jnp.float32)
    if shards:
        array = array * block_scale(rng, shape, shards, -0.22, 0.18)
    return jnp.clip(array, -most, most).astype(kind)


def setup_inputs(seed: int = 0) -> dict:
    key_list = jax.random.split(jax.random.key(seed), 6)
    return {
        "teacher_hidden": draw_teacher_hidden(jax.random.fold_in(key_list[5], 71), 0),
        "student_hidden": draw_student_hidden(jax.random.fold_in(key_list[5], 71), 0),
        "teacher_weight": normal_values(key_list[2], (DT, VOCAB), (DT // 4) ** -0.5, 0.1875, ((0, 4), (1, 64))),
        "student_weight": normal_values(key_list[3], (DS, VOCAB), (DS // 4) ** -0.5, 0.1875, ((0, 4), (1, 64))),
        "sampled_ids": touch_ends(jax.random.randint(key_list[4], (TOKENS,), 0, VOCAB), jax.random.fold_in(key_list[4], 1), 0, VOCAB - 1).astype(jnp.int32),
    }


def softcap(values):
    return 30.0 * jnp.tanh(values / 30.0)


def reference(teacher_hidden, student_hidden, teacher_weight, student_weight, sampled_ids):
    teacher_logits = softcap(jnp.dot(teacher_hidden, teacher_weight, preferred_element_type=jnp.float32))
    student_logits = softcap(jnp.dot(student_hidden, student_weight, preferred_element_type=jnp.float32))
    student_exp = jnp.exp(student_logits)
    teacher_total = jnp.sum(jnp.exp(teacher_logits), axis=1)
    student_total = jnp.sum(student_exp, axis=1)
    cross = jnp.sum(student_exp * (student_logits - teacher_logits), axis=1)
    student_log = jnp.log(student_total)
    teacher_log = jnp.log(teacher_total)
    divergence = cross / student_total - student_log + teacher_log
    columns = jnp.arange(VOCAB, dtype=jnp.int32)
    matches = columns[None, :] == sampled_ids[:, None]
    student_pick = jnp.sum(jnp.where(matches, student_logits, 0.0), axis=1)
    teacher_pick = jnp.sum(jnp.where(matches, teacher_logits, 0.0), axis=1)
    chosen = jnp.stack([student_pick - student_log, teacher_pick - teacher_log])
    probs = student_exp / student_total[:, None]
    shifted = student_logits - teacher_logits - student_log[:, None] + teacher_log[:, None] - divergence[:, None]
    logit_grad = (probs * shifted * (1.0 - (student_logits / 30.0) ** 2)).astype(jnp.bfloat16)
    weight_grad = jnp.dot(student_hidden.T, logit_grad, preferred_element_type=jnp.float32).astype(jnp.bfloat16)
    hidden_grad = jnp.dot(logit_grad, student_weight.T, preferred_element_type=jnp.float32).astype(jnp.bfloat16)
    return divergence, chosen, logit_grad, weight_grad, hidden_grad
```

```python
import jax
import jax.numpy as jnp
from jax import lax
from jax.experimental import pallas as pl
from jax.experimental.pallas import tpu as pltpu
from jax.sharding import PartitionSpec as P

MESH = pl.DeviceIdType.MESH
F32, BF16, I16 = jnp.float32, jnp.bfloat16, jnp.int16
NX, NY, NZ, NC = 4, 4, 8, 2
HALVES = 2
ROWS = 64
COLS = 2000
WIDE = 2048
TAIL = WIDE - 128
GROUP = 16
SCALE = 32000.0
BLOCKS = ((0, 512), (512, 1024), (1024, 1536), (1536, COLS))


def softcap(values):
    return 30.0 * jnp.tanh(values * (1.0 / 30.0))


def encode(values, ref, at):
    most = jnp.max(jnp.abs(values), axis=1, keepdims=True)
    power = jnp.ceil(jnp.log2(jnp.maximum(most, 1e-30)))
    whole = jnp.round(values * (jnp.exp2(-power) * SCALE))
    lane = lax.broadcasted_iota(jnp.int32, (values.shape[0], 128), 1)
    last = jnp.where(lane >= COLS - TAIL, power, whole[:, TAIL:])
    ref[at, 0:TAIL] = whole[:, :TAIL].astype(I16)
    ref[at, TAIL:WIDE] = last.astype(I16)


def decode(ref, at):
    values = ref[at, :].astype(F32)
    lane = lax.broadcasted_iota(jnp.int32, (values.shape[0], 128), 1)
    power = jnp.max(jnp.where(lane >= COLS - TAIL, values[:, TAIL:], -1000.0), axis=1, keepdims=True)
    return values * (jnp.exp2(power) * (1.0 / SCALE))


def kernel(
    th, sh, ids, wt_hbm, ws_hbm,
    kl_out, chosen_out, grad_out, wg_out, hg_out,
    wt, ws, ht, hs, lt, ls, part, one_s, one_r, two_s, two_r, logits, stat, ids_at, sr1, sr2, res, res_at, back,
    grads, wg_acc, wg_stage, hp, hc, ysum, yr, zs, zr,
    w_sem, zsnd, zrcv, ysnd, yrcv, csnd, crcv,
    one_ss, one_rs, two_ss, two_rs, s1_ss, s1_rs, s2_ss, s2_rs, g_ss, g_rs, f_ss, f_rs,
    hc_ss, hc_rs, hy_ss, hy_rs, hz_ss, hz_rs, out_sem,
):
    x = lax.axis_index("row")
    v = lax.axis_index("vocab")
    y, z, c = v // 16, (v // 2) % 8, v % 2
    right, left, across = (x + 1) % 4, (x + 3) % 4, (x + 2) % 4

    def at_x(to):
        return (to, v)

    def at_v(ty, tz, tc):
        return (x, ty * 16 + tz * 2 + tc)

    def remote(src, dst, ss, rs, device):
        return pltpu.make_async_remote_copy(
            src_ref=src, dst_ref=dst, send_sem=ss, recv_sem=rs, device_id=device, device_id_type=MESH
        )

    def landed(ref, sem):
        remote(ref, ref, sem, sem, at_x(right)).wait_recv()

    def left_here(ref, sem):
        remote(ref, ref, sem, sem, at_x(right)).wait_send()

    load_s = pltpu.make_async_copy(ws_hbm, ws, w_sem.at[0])
    load_t = pltpu.make_async_copy(wt_hbm, wt, w_sem.at[1])
    load_s.start()
    load_t.start()

    barrier = pltpu.get_barrier_semaphore()
    for to in (right, left):
        pl.semaphore_signal(barrier, inc=1, device_id=at_x(to), device_id_type=MESH)
    for step in range(1, 8):
        pl.semaphore_signal(
            barrier, inc=1, device_id=at_v((y + step // 2) % 4, z, (c + step) % 2), device_id_type=MESH
        )
        pl.semaphore_signal(barrier, inc=1, device_id=at_v(y, (z + step) % 8, c), device_id_type=MESH)

    hs[y, z, c] = sh[...]
    ht[y, z, c] = th[...]
    part[:, :, TAIL:WIDE] = jnp.zeros((3, ROWS, 128), F32)
    stat[...] = jnp.zeros((128, 128), F32)
    res[...] = jnp.zeros((128, 128), F32)
    ids_at[...] = jnp.transpose(jnp.broadcast_to(ids[...].astype(F32), (128, 128)))

    pl.semaphore_wait(barrier, 16)

    both = ((0, hs), (1, ht))
    for m, ref in both:
        for step in range(1, 8):
            to = (z + step) % 8
            remote(
                ref.at[y, z, c], ref.at[y, z, c], zsnd.at[m, step], zrcv.at[m, z], at_v(y, to, c)
            ).start()

    def z_arrive(m, ref, half):
        for k in range(4):
            zz = 4 * half + k

            @pl.when(zz != z)
            def _():
                landed(ref.at[y, zz, c], zrcv.at[m, zz])

    def y_send(m, ref, half):
        src = ref.at[y, pl.ds(4 * half, 4), c]
        for step in (1, 3, 2):
            remote(
                src, src, ysnd.at[m, half, step], yrcv.at[m, half, y], at_v((y + step) % 4, z, c)
            ).start()

    def y_arrive(m, ref, half):
        for step in (1, 3, 2):
            yy = (y + step) % 4
            landed(ref.at[yy, pl.ds(4 * half, 4), c], yrcv.at[m, half, yy])

    def c_send(m, ref, half):
        src = ref.at[:, pl.ds(4 * half, 4), c]
        remote(src, src, csnd.at[m, half], crcv.at[m, half], at_v(y, z, 1 - c)).start()

    def c_arrive(m, ref, half):
        landed(ref.at[:, pl.ds(4 * half, 4), 1 - c], crcv.at[m, half])

    def layout(m, ref, rows, half):
        wide = rows.shape[-1]
        for k in range(4):
            block = ref[k, 4 * half : 4 * half + 4].astype(F32)
            rows[half, k] = block.reshape(ROWS, wide).astype(BF16)

    def product(m, half, chunk, slot):
        rows, weight = (ls, ws) if m == 0 else (lt, wt)
        lhs = rows[half, chunk]
        for lo, hi in BLOCKS:
            part[slot, :, lo:hi] = jnp.dot(lhs, weight[:, lo:hi], preferred_element_type=F32)

    def hop_one(m, half):
        u = 2 * half + m
        product(m, half, across, 0)

        @pl.loop(0, ROWS // GROUP)
        def _(g):
            at = pl.ds(pl.multiple_of(g * GROUP, GROUP), GROUP)
            encode(part[0, at, :], one_s.at[u], at)

        remote(
            one_s.at[u, pl.ds(0, 32)], one_r.at[u, 0], one_ss.at[u, 0], one_rs.at[u, 0], at_x(right)
        ).start()
        remote(
            one_s.at[u, pl.ds(32, 32)], one_r.at[u, 1], one_ss.at[u, 1], one_rs.at[u, 1], at_x(left)
        ).start()

    def hop_two(m, half):
        u = 2 * half + m
        for side, chunk, to in ((0, right, right), (1, left, left)):
            product(m, half, chunk, 1 + side)
        for side, to in ((0, right), (1, left)):
            landed(one_r.at[u, side], one_rs.at[u, side])

            @pl.loop(0, 2)
            def _(g):
                inner = pl.ds(pl.multiple_of(g * GROUP, GROUP), GROUP)
                at = pl.ds(pl.multiple_of(side * 32 + g * GROUP, GROUP), GROUP)
                plain = pl.ds(pl.multiple_of((1 - side) * 32 + g * GROUP, GROUP), GROUP)
                encode(part[1 + side, at, :] + decode(one_r.at[u, side], inner), two_s.at[u, side], at)
                encode(part[1 + side, plain, :], two_s.at[u, side], plain)

            remote(
                two_s.at[u, side], two_r.at[u, side], two_ss.at[u, side], two_rs.at[u, side], at_x(to)
            ).start()

    def finish(m, half):
        u = 2 * half + m
        product(m, half, x, 0)
        for side in (0, 1):
            landed(two_r.at[u, side], two_rs.at[u, side])
        column = lax.broadcasted_iota(jnp.int32, (GROUP, WIDE), 1)
        lane = lax.broadcasted_iota(jnp.int32, (GROUP, 128), 1)

        @pl.loop(0, ROWS // GROUP)
        def _(g):
            at = pl.ds(pl.multiple_of(g * GROUP, GROUP), GROUP)
            raw = part[0, at, :] + decode(two_r.at[u, 0], at) + decode(two_r.at[u, 1], at)
            capped = softcap(raw)
            logits[half, m, at, :] = capped
            if m == 1:
                here = pl.ds(pl.multiple_of(half * ROWS + g * GROUP, GROUP), GROUP)
                student = logits[half, 0, at, :]
                valid = column < COLS
                t_exp = jnp.where(valid, jnp.exp(capped), 0.0)
                s_exp = jnp.where(valid, jnp.exp(student), 0.0)
                wanted = ids_at[here, 0:1].astype(jnp.int32) - v * COLS
                hit = jnp.logical_and(column == wanted, valid)
                sums = (
                    t_exp,
                    jnp.where(hit, capped, 0.0),
                    s_exp,
                    s_exp * (student - capped),
                    jnp.where(hit, student, 0.0),
                )
                tile = jnp.zeros((GROUP, 128), F32)
                for j, term in enumerate(sums):
                    tile = jnp.where(lane == j, jnp.sum(term, axis=1, keepdims=True), tile)
                stat[here, :] = tile

    group = y * 2 + c

    def stats_one(half):
        sr1[half, group] = jnp.transpose(stat[...])[0:8, :]
        for step in range(1, 8):
            remote(
                sr1.at[half, group], sr1.at[half, group], s1_ss.at[half, step], s1_rs.at[half, group],
                at_v((y + step // 2) % 4, z, (c + step) % 2),
            ).start()

    def stats_two(half):
        for step in range(1, 8):
            who = ((y + step // 2) % 4) * 2 + (c + step) % 2
            landed(sr1.at[half, who], s1_rs.at[half, who])
        total = sr1[half, 0]
        for k in range(1, 8):
            total = total + sr1[half, k]
        sr2[half, z] = total
        for step in range(1, 8):
            remote(
                sr2.at[half, z], sr2.at[half, z], s2_ss.at[half, step], s2_rs.at[half, z],
                at_v(y, (z + step) % 8, c),
            ).start()

    def gradient(half):
        for step in range(1, 8):
            who = (z + step) % 8
            landed(sr2.at[half, who], s2_rs.at[half, who])
        total = sr2[half, 0]
        for k in range(1, 8):
            total = total + sr2[half, k]
        t_total, t_pick, s_total, cross, s_pick = (total[j : j + 1, :] for j in range(5))
        s_log, t_log = jnp.log(s_total), jnp.log(t_total)
        divergence = cross / s_total - s_log + t_log
        res[0:1, :] = 1.0 / s_total
        res[1:2, :] = t_log - s_log - divergence
        back[half, 0:1, :] = divergence
        back[half, 1:2, :] = s_pick - s_log
        back[half, 2:3, :] = t_pick - t_log
        res_at[...] = jnp.transpose(res[...])

        @pl.loop(0, ROWS // GROUP)
        def _(g):
            at = pl.ds(pl.multiple_of(g * GROUP, GROUP), GROUP)
            here = pl.ds(pl.multiple_of(half * ROWS + g * GROUP, GROUP), GROUP)
            student, teacher = logits[half, 0, at, :], logits[half, 1, at, :]
            inverse, shift = res_at[here, 0:1], res_at[here, 1:2]
            ratio = student * (1.0 / 30.0)
            value = (
                jnp.exp(student) * inverse * (student - teacher + shift) * (1.0 - ratio * ratio)
            ).astype(BF16)
            grads[half, x, at, :] = value
            grad_out[here, :] = value[:, :COLS]

        mine = grads.at[half, x]
        remote(mine, mine, g_ss.at[half, 0], g_rs.at[half, 0], at_x(right)).start()
        remote(mine, mine, g_ss.at[half, 1], g_rs.at[half, 1], at_x(left)).start()

    def forward(half):
        landed(grads.at[half, left], g_rs.at[half, 0])
        src = grads.at[half, left, pl.ds(0, 32)]
        remote(src, src, f_ss.at[half, 0], f_rs.at[half, 0], at_x(right)).start()
        landed(grads.at[half, right], g_rs.at[half, 1])
        src = grads.at[half, right, pl.ds(32, 32)]
        remote(src, src, f_ss.at[half, 1], f_rs.at[half, 1], at_x(left)).start()

    def gathered(half):
        landed(grads.at[half, across, pl.ds(0, 32)], f_rs.at[half, 0])
        landed(grads.at[half, across, pl.ds(32, 32)], f_rs.at[half, 1])

    def all_rows(half):
        return grads[half, :, :, 0:COLS].reshape(NX * ROWS, COLS)

    def hidden_product(half):
        rows = all_rows(half)
        for lo, hi in ((0, 256), (256, 512), (512, 768), (768, 896)):
            block = lax.dot_general(
                rows, ws[lo:hi, :], (((1,), (1,)), ((), ())), preferred_element_type=F32
            )
            hp[half, :, :, :, :, lo:hi] = block.reshape(4, 4, 2, 8, hi - lo)
        remote(
            hp.at[half, :, :, 1 - c], hc.at[half], hc_ss.at[half], hc_rs.at[half], at_v(y, z, 1 - c)
        ).start()

    def weight_product(half):
        rows = all_rows(half)

        @pl.loop(0, 7)
        def _(i):
            at = pl.ds(pl.multiple_of(i * 128, 128), 128)
            lhs = ls[half, :, :, at].reshape(NX * ROWS, 128)
            block = lax.dot_general(lhs, rows, (((0,), (0,)), ((), ())), preferred_element_type=F32)
            if half == 0:
                wg_acc[at, :] = block
            else:
                wg_stage[at, :] = (wg_acc[at, :] + block).astype(BF16)

    def hidden_y(half):
        landed(hc.at[half], hc_rs.at[half])
        for k in range(4):
            total = hp[half, k, :, c] + hc[half, k]
            ysum[half, k] = total.reshape(32, 896).astype(BF16)
        for step in (1, 3, 2):
            to = (y + step) % 4
            remote(
                ysum.at[half, to], yr.at[half, step], hy_ss.at[half, step], hy_rs.at[half, step],
                at_v(to, z, c),
            ).start()

    def hidden_z(half):
        total = ysum[half, y].astype(F32)
        for step in (1, 2, 3):
            landed(yr.at[half, step], hy_rs.at[half, step])
            total = total + yr[half, step].astype(F32)
        zs[half] = total.reshape(4, 8, 896)
        for k in range(4):
            zz = 4 * half + k

            @pl.when(zz != z)
            def _():
                remote(
                    zs.at[half, k], zr.at[z], hz_ss.at[half, k], hz_rs.at[z], at_v(y, zz, c)
                ).start()

    def hidden_end(half):
        @pl.when(z // 4 == half)
        def _():
            zr[z] = zs[half, z % 4]
            for step in range(1, 8):
                who = (z + step) % 8
                landed(zr.at[who], hz_rs.at[who])
            total = zr[0]
            for k in range(1, 8):
                total = total + zr[k]
            hg_out[...] = total.astype(BF16)

    for m, ref in both:
        for half in range(HALVES):
            z_arrive(m, ref, half)
            y_send(m, ref, half)
    for half in range(HALVES):
        y_arrive(0, hs, half)
        c_send(0, hs, half)
    c_arrive(0, hs, 0)
    layout(0, hs, ls, 0)
    load_s.wait()
    hop_one(0, 0)
    c_arrive(0, hs, 1)
    layout(0, hs, ls, 1)
    for half in range(HALVES):
        y_arrive(1, ht, half)
        c_send(1, ht, half)
    load_t.wait()
    c_arrive(1, ht, 0)
    layout(1, ht, lt, 0)
    hop_one(1, 0)
    c_arrive(1, ht, 1)
    layout(1, ht, lt, 1)
    hop_two(0, 0)
    hop_one(0, 1)
    hop_two(1, 0)
    hop_one(1, 1)
    finish(0, 0)
    hop_two(0, 1)
    finish(1, 0)
    stats_one(0)
    hop_two(1, 1)
    stats_two(0)
    finish(0, 1)
    gradient(0)
    finish(1, 1)
    stats_one(1)
    forward(0)
    stats_two(1)
    gathered(0)
    hidden_product(0)
    gradient(1)
    hidden_y(0)
    weight_product(0)
    hidden_z(0)
    forward(1)
    hidden_end(0)
    gathered(1)
    hidden_product(1)
    weight_product(1)
    store = pltpu.make_async_copy(wg_stage, wg_out, out_sem)
    store.start()
    hidden_y(1)
    hidden_z(1)
    lane = lax.broadcasted_iota(jnp.int32, (1, 128), 1)
    kl_out[...] = jnp.where(lane < ROWS, back[0, 0:1, :], back[1, 0:1, :])
    chosen_out[...] = jnp.where(lane < ROWS, back[0, 1:3, :], back[1, 1:3, :])
    hidden_end(1)
    store.wait()

    for m, ref in both:
        for step in range(1, 8):
            left_here(ref.at[y, z, c], zsnd.at[m, step])
        for half in range(HALVES):
            for step in (1, 2, 3):
                left_here(ref.at[y, pl.ds(4 * half, 4), c], ysnd.at[m, half, step])
            left_here(ref.at[:, pl.ds(4 * half, 4), c], csnd.at[m, half])
    for u in range(4):
        for side in (0, 1):
            left_here(one_s.at[u, pl.ds(0, 32)], one_ss.at[u, side])
            left_here(two_s.at[u, side], two_ss.at[u, side])
    for half in range(HALVES):
        for step in range(1, 8):
            left_here(sr1.at[half, group], s1_ss.at[half, step])
            left_here(sr2.at[half, z], s2_ss.at[half, step])
        for side in (0, 1):
            left_here(grads.at[half, x], g_ss.at[half, side])
            left_here(grads.at[half, x, pl.ds(0, 32)], f_ss.at[half, side])
        left_here(hc.at[half], hc_ss.at[half])
        for step in (1, 2, 3):
            left_here(ysum.at[half, 0], hy_ss.at[half, step])
        for k in range(4):

            @pl.when(4 * half + k != z)
            def _():
                left_here(zs.at[half, k], hz_ss.at[half, k])


def body(teacher_hidden, student_hidden, teacher_weight, student_weight, sampled_ids):
    dma, vmem = pltpu.SemaphoreType.DMA, pltpu.VMEM
    on_chip = pl.BlockSpec(memory_space=pltpu.VMEM)
    any_space = pl.BlockSpec(memory_space=pl.ANY)
    kt, ks = teacher_weight.shape[0], student_weight.shape[0]
    outs = (
        jax.ShapeDtypeStruct((1, 128), F32),
        jax.ShapeDtypeStruct((2, 128), F32),
        jax.ShapeDtypeStruct((128, COLS), BF16),
        jax.ShapeDtypeStruct((ks, COLS), BF16),
        jax.ShapeDtypeStruct((8, ks), BF16),
    )
    kl, chosen, grad, weight_grad, hidden_grad = pl.pallas_call(
        kernel,
        out_shape=outs,
        in_specs=[on_chip, on_chip, on_chip, any_space, any_space],
        out_specs=(on_chip, on_chip, on_chip, any_space, on_chip),
        scratch_shapes=[
            vmem((kt, COLS), BF16), vmem((ks, COLS), BF16),
            vmem((4, 8, 2, 8, kt), BF16), vmem((4, 8, 2, 8, ks), BF16),
            vmem((2, 4, ROWS, kt), BF16), vmem((2, 4, ROWS, ks), BF16),
            vmem((3, ROWS, WIDE), F32),
            vmem((4, ROWS, WIDE), I16), vmem((4, 2, 32, WIDE), I16),
            vmem((4, 2, ROWS, WIDE), I16), vmem((4, 2, ROWS, WIDE), I16),
            vmem((2, 2, ROWS, WIDE), F32),
            vmem((128, 128), F32), vmem((128, 128), F32),
            vmem((2, 8, 8, 128), F32), vmem((2, 8, 8, 128), F32),
            vmem((128, 128), F32), vmem((128, 128), F32), vmem((2, 8, 128), F32),
            vmem((2, 4, ROWS, WIDE), BF16),
            vmem((ks, COLS), F32), vmem((ks, COLS), BF16),
            vmem((2, 4, 4, 2, 8, ks), F32), vmem((2, 4, 4, 8, ks), F32),
            vmem((2, 4, 32, ks), BF16), vmem((2, 4, 32, ks), BF16),
            vmem((2, 4, 8, ks), F32), vmem((8, 8, ks), F32),
            dma((2,)), dma((2, 8)), dma((2, 8)), dma((2, 2, 4)), dma((2, 2, 4)), dma((2, 2)), dma((2, 2)),
            dma((4, 2)), dma((4, 2)), dma((4, 2)), dma((4, 2)),
            dma((2, 8)), dma((2, 8)), dma((2, 8)), dma((2, 8)),
            dma((2, 2)), dma((2, 2)), dma((2, 2)), dma((2, 2)),
            dma((2,)), dma((2,)), dma((2, 4)), dma((2, 4)), dma((2, 4)), dma((8,)), dma(()),
        ],
        compiler_params=pltpu.CompilerParams(
            collective_id=0, has_side_effects=True, vmem_limit_bytes=60 * 1024 * 1024
        ),
    )(teacher_hidden, student_hidden, sampled_ids.reshape(1, 128), teacher_weight, student_weight)
    return kl.reshape(128), chosen, grad, weight_grad, hidden_grad


def solution(mesh):
    placed = (P("vocab", "row"), P("vocab", "row"), P("row", "vocab"), P("row", "vocab"), P("row"))
    return jax.shard_map(
        body,
        mesh=mesh,
        in_specs=placed,
        out_specs=(P("row"), P(None, "row"), P("row", "vocab"), P("row", "vocab"), P("vocab", "row")),
        check_vma=False,
    )
```

```python
import jax
import jax.numpy as jnp
from jax import lax
from jax.experimental import pallas as pl
from jax.experimental.pallas import tpu as pltpu
from jax.sharding import PartitionSpec as P

MESH = pl.DeviceIdType.MESH
F32, BF16, I16 = jnp.float32, jnp.bfloat16, jnp.int16
NX, NY, NZ, NC = 4, 4, 8, 2
HALVES = 2
ROWS = 64
COLS = 2000
WIDE = 2048
TAIL = WIDE - 128
GROUP = 16
SCALE = 32000.0
BLOCKS = ((0, 512), (512, 1024), (1024, 1536), (1536, COLS))


def softcap(values):
    return 30.0 * jnp.tanh(values * (1.0 / 30.0))


def encode(values, ref, at):
    most = jnp.max(jnp.abs(values), axis=1, keepdims=True)
    power = jnp.ceil(jnp.log2(jnp.maximum(most, 1e-30)))
    whole = jnp.round(values * (jnp.exp2(-power) * SCALE))
    lane = lax.broadcasted_iota(jnp.int32, (values.shape[0], 128), 1)
    last = jnp.where(lane >= COLS - TAIL, power, whole[:, TAIL:])
    ref[at, 0:TAIL] = whole[:, :TAIL].astype(I16)
    ref[at, TAIL:WIDE] = last.astype(I16)


def decode(ref, at):
    values = ref[at, :].astype(F32)
    lane = lax.broadcasted_iota(jnp.int32, (values.shape[0], 128), 1)
    power = jnp.max(jnp.where(lane >= COLS - TAIL, values[:, TAIL:], -1000.0), axis=1, keepdims=True)
    return values * (jnp.exp2(power) * (1.0 / SCALE))


def kernel(
    th, sh, ids, wt_hbm, ws_hbm,
    kl_out, chosen_out, grad_out, wg_out, hg_out,
    wt, ws, ht, hs, lt, ls, part, one_s, one_r, two_s, two_r, logits, stat, ids_at, sr1, sr2, res, res_at, back,
    grads, wg_acc, wg_stage, grad_stage, hp, hc, ysum, yr, zs, zr,
    w_sem, zsnd, zrcv, ysnd, yrcv, csnd, crcv,
    one_ss, one_rs, two_ss, two_rs, s1_ss, s1_rs, s2_ss, s2_rs, g_ss, g_rs, f_ss, f_rs,
    hc_ss, hc_rs, hy_ss, hy_rs, hz_ss, hz_rs, out_sem,
):
    x = lax.axis_index("row")
    v = lax.axis_index("vocab")
    y, z, c = v // 16, (v // 2) % 8, v % 2
    right, left, across = (x + 1) % 4, (x + 3) % 4, (x + 2) % 4

    def at_x(to):
        return (to, v)

    def at_v(ty, tz, tc):
        return (x, ty * 16 + tz * 2 + tc)

    def remote(src, dst, ss, rs, device):
        return pltpu.make_async_remote_copy(
            src_ref=src, dst_ref=dst, send_sem=ss, recv_sem=rs, device_id=device, device_id_type=MESH
        )

    def landed(ref, sem):
        remote(ref, ref, sem, sem, at_x(right)).wait_recv()

    def left_here(ref, sem):
        remote(ref, ref, sem, sem, at_x(right)).wait_send()

    load_s = pltpu.make_async_copy(ws_hbm, ws, w_sem.at[0])
    load_t = pltpu.make_async_copy(wt_hbm, wt, w_sem.at[1])
    load_s.start()
    load_t.start()

    barrier = pltpu.get_barrier_semaphore()
    for to in (right, left):
        pl.semaphore_signal(barrier, inc=1, device_id=at_x(to), device_id_type=MESH)
    for step in range(1, 8):
        pl.semaphore_signal(
            barrier, inc=1, device_id=at_v((y + step // 2) % 4, z, (c + step) % 2), device_id_type=MESH
        )
        pl.semaphore_signal(barrier, inc=1, device_id=at_v(y, (z + step) % 8, c), device_id_type=MESH)

    hs[y, z, c] = sh[...]
    ht[y, z, c] = th[...]
    part[:, :, TAIL:WIDE] = jnp.zeros((3, ROWS, 128), F32)
    stat[...] = jnp.zeros((128, 128), F32)
    res[...] = jnp.zeros((128, 128), F32)
    ids_at[...] = jnp.transpose(jnp.broadcast_to(ids[...].astype(F32), (128, 128)))

    pl.semaphore_wait(barrier, 16)

    both = ((0, hs), (1, ht))
    for m, ref in both:
        for step in range(1, 8):
            to = (z + step) % 8
            remote(
                ref.at[y, z, c], ref.at[y, z, c], zsnd.at[m, step], zrcv.at[m, z], at_v(y, to, c)
            ).start()

    def z_arrive(m, ref, half):
        for k in range(4):
            zz = 4 * half + k

            @pl.when(zz != z)
            def _():
                landed(ref.at[y, zz, c], zrcv.at[m, zz])

    def y_send(m, ref, half):
        src = ref.at[y, pl.ds(4 * half, 4), c]
        for step in (1, 3, 2):
            remote(
                src, src, ysnd.at[m, half, step], yrcv.at[m, half, y], at_v((y + step) % 4, z, c)
            ).start()

    def y_arrive(m, ref, half):
        for step in (1, 3, 2):
            yy = (y + step) % 4
            landed(ref.at[yy, pl.ds(4 * half, 4), c], yrcv.at[m, half, yy])

    def c_send(m, ref, half):
        src = ref.at[:, pl.ds(4 * half, 4), c]
        remote(src, src, csnd.at[m, half], crcv.at[m, half], at_v(y, z, 1 - c)).start()

    def c_arrive(m, ref, half):
        landed(ref.at[:, pl.ds(4 * half, 4), 1 - c], crcv.at[m, half])

    def layout(m, ref, rows, half):
        wide = rows.shape[-1]
        for k in range(4):
            block = ref[k, 4 * half : 4 * half + 4].astype(F32)
            rows[half, k] = block.reshape(ROWS, wide).astype(BF16)

    def product(m, half, chunk, slot):
        rows, weight = (ls, ws) if m == 0 else (lt, wt)
        lhs = rows[half, chunk]
        for lo, hi in BLOCKS:
            part[slot, :, lo:hi] = lax.dot_general(
                lhs, weight[lo:hi, :], (((1,), (1,)), ((), ())), preferred_element_type=F32
            )

    def hop_one(m, half):
        u = 2 * half + m
        product(m, half, across, 0)

        @pl.loop(0, ROWS // GROUP)
        def _(g):
            at = pl.ds(pl.multiple_of(g * GROUP, GROUP), GROUP)
            encode(part[0, at, :], one_s.at[u], at)

        remote(
            one_s.at[u, pl.ds(0, 32)], one_r.at[u, 0], one_ss.at[u, 0], one_rs.at[u, 0], at_x(right)
        ).start()
        remote(
            one_s.at[u, pl.ds(32, 32)], one_r.at[u, 1], one_ss.at[u, 1], one_rs.at[u, 1], at_x(left)
        ).start()

    def hop_two(m, half):
        u = 2 * half + m
        for side, chunk, to in ((0, right, right), (1, left, left)):
            product(m, half, chunk, 1 + side)
        for side, to in ((0, right), (1, left)):
            landed(one_r.at[u, side], one_rs.at[u, side])

            @pl.loop(0, 2)
            def _(g):
                inner = pl.ds(pl.multiple_of(g * GROUP, GROUP), GROUP)
                at = pl.ds(pl.multiple_of(side * 32 + g * GROUP, GROUP), GROUP)
                plain = pl.ds(pl.multiple_of((1 - side) * 32 + g * GROUP, GROUP), GROUP)
                encode(part[1 + side, at, :] + decode(one_r.at[u, side], inner), two_s.at[u, side], at)
                encode(part[1 + side, plain, :], two_s.at[u, side], plain)

            remote(
                two_s.at[u, side], two_r.at[u, side], two_ss.at[u, side], two_rs.at[u, side], at_x(to)
            ).start()

    def finish(m, half):
        u = 2 * half + m
        product(m, half, x, 0)
        for side in (0, 1):
            landed(two_r.at[u, side], two_rs.at[u, side])
        column = lax.broadcasted_iota(jnp.int32, (GROUP, WIDE), 1)
        lane = lax.broadcasted_iota(jnp.int32, (GROUP, 128), 1)

        @pl.loop(0, ROWS // GROUP)
        def _(g):
            at = pl.ds(pl.multiple_of(g * GROUP, GROUP), GROUP)
            raw = part[0, at, :] + decode(two_r.at[u, 0], at) + decode(two_r.at[u, 1], at)
            capped = softcap(raw)
            logits[half, m, at, :] = capped
            if m == 1:
                here = pl.ds(pl.multiple_of(half * ROWS + g * GROUP, GROUP), GROUP)
                student = logits[half, 0, at, :]
                valid = column < COLS
                t_exp = jnp.where(valid, jnp.exp(capped), 0.0)
                s_exp = jnp.where(valid, jnp.exp(student), 0.0)
                wanted = ids_at[here, 0:1].astype(jnp.int32) - v * COLS
                hit = jnp.logical_and(column == wanted, valid)
                sums = (
                    t_exp,
                    jnp.where(hit, capped, 0.0),
                    s_exp,
                    s_exp * (student - capped),
                    jnp.where(hit, student, 0.0),
                )
                tile = jnp.zeros((GROUP, 128), F32)
                for j, term in enumerate(sums):
                    tile = jnp.where(lane == j, jnp.sum(term, axis=1, keepdims=True), tile)
                stat[here, :] = tile

    group = y * 2 + c

    def stats_one(half):
        sr1[half, group] = jnp.transpose(stat[...])[0:8, :]
        for step in range(1, 8):
            remote(
                sr1.at[half, group], sr1.at[half, group], s1_ss.at[half, step], s1_rs.at[half, group],
                at_v((y + step // 2) % 4, z, (c + step) % 2),
            ).start()

    def stats_two(half):
        for step in range(1, 8):
            who = ((y + step // 2) % 4) * 2 + (c + step) % 2
            landed(sr1.at[half, who], s1_rs.at[half, who])
        total = sr1[half, 0]
        for k in range(1, 8):
            total = total + sr1[half, k]
        sr2[half, z] = total
        for step in range(1, 8):
            remote(
                sr2.at[half, z], sr2.at[half, z], s2_ss.at[half, step], s2_rs.at[half, z],
                at_v(y, (z + step) % 8, c),
            ).start()

    def gradient(half):
        for step in range(1, 8):
            who = (z + step) % 8
            landed(sr2.at[half, who], s2_rs.at[half, who])
        total = sr2[half, 0]
        for k in range(1, 8):
            total = total + sr2[half, k]
        t_total, t_pick, s_total, cross, s_pick = (total[j : j + 1, :] for j in range(5))
        s_log, t_log = jnp.log(s_total), jnp.log(t_total)
        divergence = cross / s_total - s_log + t_log
        res[0:1, :] = 1.0 / s_total
        res[1:2, :] = t_log - s_log - divergence
        back[half, 0:1, :] = divergence
        back[half, 1:2, :] = s_pick - s_log
        back[half, 2:3, :] = t_pick - t_log
        res_at[...] = jnp.transpose(res[...])

        @pl.loop(0, ROWS // GROUP)
        def _(g):
            at = pl.ds(pl.multiple_of(g * GROUP, GROUP), GROUP)
            here = pl.ds(pl.multiple_of(half * ROWS + g * GROUP, GROUP), GROUP)
            student, teacher = logits[half, 0, at, :], logits[half, 1, at, :]
            inverse, shift = res_at[here, 0:1], res_at[here, 1:2]
            ratio = student * (1.0 / 30.0)
            value = (
                jnp.exp(student) * inverse * (student - teacher + shift) * (1.0 - ratio * ratio)
            ).astype(BF16)
            grads[half, x, at, :] = value

        mine = grads.at[half, x]
        remote(mine, mine, g_ss.at[half, 0], g_rs.at[half, 0], at_x(right)).start()
        remote(mine, mine, g_ss.at[half, 1], g_rs.at[half, 1], at_x(left)).start()

    def forward(half):
        landed(grads.at[half, left], g_rs.at[half, 0])
        src = grads.at[half, left, pl.ds(0, 32)]
        remote(src, src, f_ss.at[half, 0], f_rs.at[half, 0], at_x(right)).start()
        landed(grads.at[half, right], g_rs.at[half, 1])
        src = grads.at[half, right, pl.ds(32, 32)]
        remote(src, src, f_ss.at[half, 1], f_rs.at[half, 1], at_x(left)).start()

    def gathered(half):
        landed(grads.at[half, across, pl.ds(0, 32)], f_rs.at[half, 0])
        landed(grads.at[half, across, pl.ds(32, 32)], f_rs.at[half, 1])

    def all_rows(half):
        return grads[half, :, :, 0:COLS].reshape(NX * ROWS, COLS)

    def hidden_product(half):
        rows = all_rows(half)
        for lo, hi in ((0, 256), (256, 512), (512, 768), (768, 896)):
            block = jnp.dot(rows, ws[:, lo:hi], preferred_element_type=F32)
            hp[half, :, :, :, :, lo:hi] = block.reshape(4, 4, 2, 8, hi - lo)
        remote(
            hp.at[half, :, :, 1 - c], hc.at[half], hc_ss.at[half], hc_rs.at[half], at_v(y, z, 1 - c)
        ).start()

    def weight_product(half):
        rows = ls[half].reshape(NX * ROWS, ls.shape[-1])

        @pl.loop(0, WIDE // 256)
        def _(i):
            at = pl.ds(pl.multiple_of(i * 256, 256), 256)
            lhs = grads[half, :, :, at].reshape(NX * ROWS, 256)
            block = lax.dot_general(lhs, rows, (((0,), (0,)), ((), ())), preferred_element_type=F32)
            if half == 0:
                wg_acc[at, :] = block
            else:
                wg_stage[at, :] = (wg_acc[at, :] + block).astype(BF16)

    def own_gradient():
        @pl.loop(0, WIDE // 128)
        def _(i):
            at = pl.ds(pl.multiple_of(i * 128, 128), 128)
            block = jnp.concatenate([grads[0, x, :, at], grads[1, x, :, at]], axis=0)
            grad_stage[at, :] = jnp.transpose(block.astype(F32)).astype(BF16)

    def hidden_y(half):
        landed(hc.at[half], hc_rs.at[half])
        for k in range(4):
            total = hp[half, k, :, c] + hc[half, k]
            ysum[half, k] = total.reshape(32, 896).astype(BF16)
        for step in (1, 3, 2):
            to = (y + step) % 4
            remote(
                ysum.at[half, to], yr.at[half, step], hy_ss.at[half, step], hy_rs.at[half, step],
                at_v(to, z, c),
            ).start()

    def hidden_z(half):
        total = ysum[half, y].astype(F32)
        for step in (1, 2, 3):
            landed(yr.at[half, step], hy_rs.at[half, step])
            total = total + yr[half, step].astype(F32)
        zs[half] = total.reshape(4, 8, 896)
        for k in range(4):
            zz = 4 * half + k

            @pl.when(zz != z)
            def _():
                remote(
                    zs.at[half, k], zr.at[z], hz_ss.at[half, k], hz_rs.at[z], at_v(y, zz, c)
                ).start()

    def hidden_end(half):
        @pl.when(z // 4 == half)
        def _():
            zr[z] = zs[half, z % 4]
            for step in range(1, 8):
                who = (z + step) % 8
                landed(zr.at[who], hz_rs.at[who])
            total = zr[0]
            for k in range(1, 8):
                total = total + zr[k]
            hg_out[...] = total.astype(BF16)

    for m, ref in both:
        for half in range(HALVES):
            z_arrive(m, ref, half)
            y_send(m, ref, half)
    for half in range(HALVES):
        y_arrive(0, hs, half)
        c_send(0, hs, half)
    c_arrive(0, hs, 0)
    layout(0, hs, ls, 0)
    load_s.wait()
    hop_one(0, 0)
    c_arrive(0, hs, 1)
    layout(0, hs, ls, 1)
    for half in range(HALVES):
        y_arrive(1, ht, half)
        c_send(1, ht, half)
    load_t.wait()
    c_arrive(1, ht, 0)
    layout(1, ht, lt, 0)
    hop_one(1, 0)
    c_arrive(1, ht, 1)
    layout(1, ht, lt, 1)
    hop_two(0, 0)
    hop_one(0, 1)
    hop_two(1, 0)
    hop_one(1, 1)
    finish(0, 0)
    hop_two(0, 1)
    finish(1, 0)
    stats_one(0)
    hop_two(1, 1)
    stats_two(0)
    finish(0, 1)
    gradient(0)
    finish(1, 1)
    stats_one(1)
    forward(0)
    stats_two(1)
    gathered(0)
    hidden_product(0)
    gradient(1)
    hidden_y(0)
    weight_product(0)
    hidden_z(0)
    forward(1)
    hidden_end(0)
    gathered(1)
    hidden_product(1)
    weight_product(1)
    store = pltpu.make_async_copy(wg_stage.at[pl.ds(0, COLS)], wg_out, out_sem.at[0])
    store.start()
    hidden_y(1)
    own_gradient()
    store_grad = pltpu.make_async_copy(grad_stage.at[pl.ds(0, COLS)], grad_out, out_sem.at[1])
    store_grad.start()
    hidden_z(1)
    lane = lax.broadcasted_iota(jnp.int32, (1, 128), 1)
    kl_out[...] = jnp.where(lane < ROWS, back[0, 0:1, :], back[1, 0:1, :])
    chosen_out[...] = jnp.where(lane < ROWS, back[0, 1:3, :], back[1, 1:3, :])
    hidden_end(1)
    store.wait()
    store_grad.wait()

    for m, ref in both:
        for step in range(1, 8):
            left_here(ref.at[y, z, c], zsnd.at[m, step])
        for half in range(HALVES):
            for step in (1, 2, 3):
                left_here(ref.at[y, pl.ds(4 * half, 4), c], ysnd.at[m, half, step])
            left_here(ref.at[:, pl.ds(4 * half, 4), c], csnd.at[m, half])
    for u in range(4):
        for side in (0, 1):
            left_here(one_s.at[u, pl.ds(0, 32)], one_ss.at[u, side])
            left_here(two_s.at[u, side], two_ss.at[u, side])
    for half in range(HALVES):
        for step in range(1, 8):
            left_here(sr1.at[half, group], s1_ss.at[half, step])
            left_here(sr2.at[half, z], s2_ss.at[half, step])
        for side in (0, 1):
            left_here(grads.at[half, x], g_ss.at[half, side])
            left_here(grads.at[half, x, pl.ds(0, 32)], f_ss.at[half, side])
        left_here(hc.at[half], hc_ss.at[half])
        for step in (1, 2, 3):
            left_here(ysum.at[half, 0], hy_ss.at[half, step])
        for k in range(4):

            @pl.when(4 * half + k != z)
            def _():
                left_here(zs.at[half, k], hz_ss.at[half, k])


def body(teacher_hidden, student_hidden, teacher_weight, student_weight, sampled_ids):
    dma, vmem = pltpu.SemaphoreType.DMA, pltpu.VMEM
    on_chip = pl.BlockSpec(memory_space=pltpu.VMEM)
    any_space = pl.BlockSpec(memory_space=pl.ANY)
    kt, ks = teacher_weight.shape[0], student_weight.shape[0]
    outs = (
        jax.ShapeDtypeStruct((1, 128), F32),
        jax.ShapeDtypeStruct((2, 128), F32),
        jax.ShapeDtypeStruct((COLS, 128), BF16),
        jax.ShapeDtypeStruct((COLS, ks), BF16),
        jax.ShapeDtypeStruct((8, ks), BF16),
    )
    kl, chosen, grad, weight_grad, hidden_grad = pl.pallas_call(
        kernel,
        out_shape=outs,
        in_specs=[on_chip, on_chip, on_chip, any_space, any_space],
        out_specs=(on_chip, on_chip, any_space, any_space, on_chip),
        scratch_shapes=[
            vmem((COLS, kt), BF16), vmem((COLS, ks), BF16),
            vmem((4, 8, 2, 8, kt), BF16), vmem((4, 8, 2, 8, ks), BF16),
            vmem((2, 4, ROWS, kt), BF16), vmem((2, 4, ROWS, ks), BF16),
            vmem((3, ROWS, WIDE), F32),
            vmem((4, ROWS, WIDE), I16), vmem((4, 2, 32, WIDE), I16),
            vmem((4, 2, ROWS, WIDE), I16), vmem((4, 2, ROWS, WIDE), I16),
            vmem((2, 2, ROWS, WIDE), F32),
            vmem((128, 128), F32), vmem((128, 128), F32),
            vmem((2, 8, 8, 128), F32), vmem((2, 8, 8, 128), F32),
            vmem((128, 128), F32), vmem((128, 128), F32), vmem((2, 8, 128), F32),
            vmem((2, 4, ROWS, WIDE), BF16),
            vmem((WIDE, ks), F32), vmem((WIDE, ks), BF16), vmem((WIDE, 128), BF16),
            vmem((2, 4, 4, 2, 8, ks), F32), vmem((2, 4, 4, 8, ks), F32),
            vmem((2, 4, 32, ks), BF16), vmem((2, 4, 32, ks), BF16),
            vmem((2, 4, 8, ks), F32), vmem((8, 8, ks), F32),
            dma((2,)), dma((2, 8)), dma((2, 8)), dma((2, 2, 4)), dma((2, 2, 4)), dma((2, 2)), dma((2, 2)),
            dma((4, 2)), dma((4, 2)), dma((4, 2)), dma((4, 2)),
            dma((2, 8)), dma((2, 8)), dma((2, 8)), dma((2, 8)),
            dma((2, 2)), dma((2, 2)), dma((2, 2)), dma((2, 2)),
            dma((2,)), dma((2,)), dma((2, 4)), dma((2, 4)), dma((2, 4)), dma((8,)), dma((2,)),
        ],
        compiler_params=pltpu.CompilerParams(
            collective_id=0, has_side_effects=True, vmem_limit_bytes=60 * 1024 * 1024
        ),
    )(teacher_hidden, student_hidden, sampled_ids.reshape(1, 128), teacher_weight.T, student_weight.T)
    return kl.reshape(128), chosen, grad.T, weight_grad.T, hidden_grad


def solution(mesh):
    placed = (P("vocab", "row"), P("vocab", "row"), P("row", "vocab"), P("row", "vocab"), P("row"))
    return jax.shard_map(
        body,
        mesh=mesh,
        in_specs=placed,
        out_specs=(P("row"), P(None, "row"), P("row", "vocab"), P("row", "vocab"), P("vocab", "row")),
        check_vma=False,
    )
```

```python
import jax
import jax.numpy as jnp
from jax import lax
from jax.experimental import pallas as pl
from jax.experimental.pallas import tpu as pltpu
from jax.sharding import PartitionSpec as P

MESH = pl.DeviceIdType.MESH
F32, BF16, I16 = jnp.float32, jnp.bfloat16, jnp.int16
NX, NY, NZ, NC = 4, 4, 8, 2
HALVES = 2
ROWS = 64
COLS = 2000
WIDE = 2048
TAIL = WIDE - 128
GROUP = 16
SCALE = 32000.0
BLOCKS = ((0, 512), (512, 1024), (1024, 1536), (1536, COLS))


def softcap(values):
    return 30.0 * jnp.tanh(values * (1.0 / 30.0))


def encode(values, ref, at):
    most = jnp.max(jnp.abs(values), axis=1, keepdims=True)
    power = jnp.ceil(jnp.log2(jnp.maximum(most, 1e-30)))
    whole = jnp.round(values * (jnp.exp2(-power) * SCALE))
    lane = lax.broadcasted_iota(jnp.int32, (values.shape[0], 128), 1)
    last = jnp.where(lane >= COLS - TAIL, power, whole[:, TAIL:])
    ref[at, 0:TAIL] = whole[:, :TAIL].astype(I16)
    ref[at, TAIL:WIDE] = last.astype(I16)


def decode(ref, at):
    values = ref[at, :].astype(F32)
    lane = lax.broadcasted_iota(jnp.int32, (values.shape[0], 128), 1)
    power = jnp.max(jnp.where(lane >= COLS - TAIL, values[:, TAIL:], -1000.0), axis=1, keepdims=True)
    return values * (jnp.exp2(power) * (1.0 / SCALE))


def kernel(
    th, sh, ids, wt_hbm, ws_hbm,
    kl_out, chosen_out, grad_out, wg_out, hg_out,
    wt, ws, ht, hs, lt, ls, part, one_s, one_r, two_s, two_r, logits, stat, ids_at, sr1, sr2, res, res_at, back,
    grads, wg_acc, wg_stage, grad_stage, hp, hc, ysum, yr, zs, zr,
    w_sem, zsnd, zrcv, ysnd, yrcv, csnd, crcv,
    one_ss, one_rs, two_ss, two_rs, s1_ss, s1_rs, s2_ss, s2_rs, g_ss, g_rs, f_ss, f_rs,
    hc_ss, hc_rs, hy_ss, hy_rs, hz_ss, hz_rs, out_sem,
):
    x = lax.axis_index("row")
    v = lax.axis_index("vocab")
    y, z, c = v // 16, (v // 2) % 8, v % 2
    right, left, across = (x + 1) % 4, (x + 3) % 4, (x + 2) % 4

    def at_x(to):
        return (to, v)

    def at_v(ty, tz, tc):
        return (x, ty * 16 + tz * 2 + tc)

    def remote(src, dst, ss, rs, device):
        return pltpu.make_async_remote_copy(
            src_ref=src, dst_ref=dst, send_sem=ss, recv_sem=rs, device_id=device, device_id_type=MESH
        )

    def landed(ref, sem):
        remote(ref, ref, sem, sem, at_x(right)).wait_recv()

    def left_here(ref, sem):
        remote(ref, ref, sem, sem, at_x(right)).wait_send()

    load_s = pltpu.make_async_copy(ws_hbm, ws, w_sem.at[0])
    load_t = pltpu.make_async_copy(wt_hbm, wt, w_sem.at[1])
    load_s.start()
    load_t.start()

    barrier = pltpu.get_barrier_semaphore()
    for to in (right, left):
        pl.semaphore_signal(barrier, inc=1, device_id=at_x(to), device_id_type=MESH)
    for step in range(1, 8):
        pl.semaphore_signal(
            barrier, inc=1, device_id=at_v((y + step // 2) % 4, z, (c + step) % 2), device_id_type=MESH
        )
        pl.semaphore_signal(barrier, inc=1, device_id=at_v(y, (z + step) % 8, c), device_id_type=MESH)

    hs[y, z, c] = sh[...]
    ht[y, z, c] = th[...]
    part[:, :, TAIL:WIDE] = jnp.zeros((3, ROWS, 128), F32)
    stat[...] = jnp.zeros((128, 128), F32)
    res[...] = jnp.zeros((128, 128), F32)
    ids_at[...] = jnp.transpose(jnp.broadcast_to(ids[...].astype(F32), (128, 128)))

    pl.semaphore_wait(barrier, 16)

    both = ((0, hs), (1, ht))
    for m, ref in both:
        for step in range(1, 8):
            to = (z + step) % 8
            remote(
                ref.at[y, z, c], ref.at[y, z, c], zsnd.at[m, step], zrcv.at[m, z], at_v(y, to, c)
            ).start()

    def z_arrive(m, ref, half):
        for k in range(4):
            zz = 4 * half + k

            @pl.when(zz != z)
            def _():
                landed(ref.at[y, zz, c], zrcv.at[m, zz])

    def y_send(m, ref, half):
        src = ref.at[y, pl.ds(4 * half, 4), c]
        for step in (1, 3, 2):
            remote(
                src, src, ysnd.at[m, half, step], yrcv.at[m, half, y], at_v((y + step) % 4, z, c)
            ).start()

    def y_arrive(m, ref, half):
        for step in (1, 3, 2):
            yy = (y + step) % 4
            landed(ref.at[yy, pl.ds(4 * half, 4), c], yrcv.at[m, half, yy])

    def c_send(m, ref, half):
        src = ref.at[:, pl.ds(4 * half, 4), c]
        remote(src, src, csnd.at[m, half], crcv.at[m, half], at_v(y, z, 1 - c)).start()

    def c_arrive(m, ref, half):
        landed(ref.at[:, pl.ds(4 * half, 4), 1 - c], crcv.at[m, half])

    def layout(m, ref, rows, half):
        wide = rows.shape[-1]
        for k in range(4):
            block = ref[k, 4 * half : 4 * half + 4].astype(F32)
            rows[half, k] = block.reshape(ROWS, wide).astype(BF16)

    def product(m, half, chunk, slot):
        rows, weight = (ls, ws) if m == 0 else (lt, wt)
        lhs = rows[half, chunk]
        for lo, hi in BLOCKS:
            part[slot, :, lo:hi] = lax.dot_general(
                lhs, weight[lo:hi, :], (((1,), (1,)), ((), ())), preferred_element_type=F32
            )

    def hop_one(m, half):
        u = 2 * half + m
        product(m, half, across, 0)

        @pl.loop(0, ROWS // GROUP)
        def _(g):
            at = pl.ds(pl.multiple_of(g * GROUP, GROUP), GROUP)
            encode(part[0, at, :], one_s.at[u], at)

        remote(
            one_s.at[u, pl.ds(0, 32)], one_r.at[u, 0], one_ss.at[u, 0], one_rs.at[u, 0], at_x(right)
        ).start()
        remote(
            one_s.at[u, pl.ds(32, 32)], one_r.at[u, 1], one_ss.at[u, 1], one_rs.at[u, 1], at_x(left)
        ).start()

    def hop_two(m, half):
        u = 2 * half + m
        for side, chunk, to in ((0, right, right), (1, left, left)):
            product(m, half, chunk, 1 + side)
        for side, to in ((0, right), (1, left)):
            landed(one_r.at[u, side], one_rs.at[u, side])

            @pl.loop(0, 2)
            def _(g):
                inner = pl.ds(pl.multiple_of(g * GROUP, GROUP), GROUP)
                at = pl.ds(pl.multiple_of(side * 32 + g * GROUP, GROUP), GROUP)
                plain = pl.ds(pl.multiple_of((1 - side) * 32 + g * GROUP, GROUP), GROUP)
                encode(part[1 + side, at, :] + decode(one_r.at[u, side], inner), two_s.at[u, side], at)
                encode(part[1 + side, plain, :], two_s.at[u, side], plain)

            remote(
                two_s.at[u, side], two_r.at[u, side], two_ss.at[u, side], two_rs.at[u, side], at_x(to)
            ).start()

    def finish(m, half):
        u = 2 * half + m
        product(m, half, x, 0)
        for side in (0, 1):
            landed(two_r.at[u, side], two_rs.at[u, side])
        column = lax.broadcasted_iota(jnp.int32, (GROUP, WIDE), 1)
        lane = lax.broadcasted_iota(jnp.int32, (GROUP, 128), 1)

        @pl.loop(0, ROWS // GROUP)
        def _(g):
            at = pl.ds(pl.multiple_of(g * GROUP, GROUP), GROUP)
            raw = part[0, at, :] + decode(two_r.at[u, 0], at) + decode(two_r.at[u, 1], at)
            capped = softcap(raw)
            logits[half, m, at, :] = capped
            if m == 1:
                here = pl.ds(pl.multiple_of(half * ROWS + g * GROUP, GROUP), GROUP)
                student = logits[half, 0, at, :]
                valid = column < COLS
                t_exp = jnp.where(valid, jnp.exp(capped), 0.0)
                s_exp = jnp.where(valid, jnp.exp(student), 0.0)
                wanted = ids_at[here, 0:1].astype(jnp.int32) - v * COLS
                hit = jnp.logical_and(column == wanted, valid)
                sums = (
                    t_exp,
                    jnp.where(hit, capped, 0.0),
                    s_exp,
                    s_exp * (student - capped),
                    jnp.where(hit, student, 0.0),
                )
                tile = jnp.zeros((GROUP, 128), F32)
                for j, term in enumerate(sums):
                    tile = jnp.where(lane == j, jnp.sum(term, axis=1, keepdims=True), tile)
                stat[here, :] = tile

    group = y * 2 + c

    def stats_one(half):
        sr1[half, group] = jnp.transpose(stat[...])[0:8, :]
        for step in range(1, 8):
            remote(
                sr1.at[half, group], sr1.at[half, group], s1_ss.at[half, step], s1_rs.at[half, group],
                at_v((y + step // 2) % 4, z, (c + step) % 2),
            ).start()

    def stats_two(half):
        for step in range(1, 8):
            who = ((y + step // 2) % 4) * 2 + (c + step) % 2
            landed(sr1.at[half, who], s1_rs.at[half, who])
        total = sr1[half, 0]
        for k in range(1, 8):
            total = total + sr1[half, k]
        sr2[half, z] = total
        for step in range(1, 8):
            remote(
                sr2.at[half, z], sr2.at[half, z], s2_ss.at[half, step], s2_rs.at[half, z],
                at_v(y, (z + step) % 8, c),
            ).start()

    def gradient(half):
        for step in range(1, 8):
            who = (z + step) % 8
            landed(sr2.at[half, who], s2_rs.at[half, who])
        total = sr2[half, 0]
        for k in range(1, 8):
            total = total + sr2[half, k]
        t_total, t_pick, s_total, cross, s_pick = (total[j : j + 1, :] for j in range(5))
        s_log, t_log = jnp.log(s_total), jnp.log(t_total)
        divergence = cross / s_total - s_log + t_log
        res[0:1, :] = 1.0 / s_total
        res[1:2, :] = t_log - s_log - divergence
        back[half, 0:1, :] = divergence
        back[half, 1:2, :] = s_pick - s_log
        back[half, 2:3, :] = t_pick - t_log
        res_at[...] = jnp.transpose(res[...])

        @pl.loop(0, ROWS // GROUP)
        def _(g):
            at = pl.ds(pl.multiple_of(g * GROUP, GROUP), GROUP)
            here = pl.ds(pl.multiple_of(half * ROWS + g * GROUP, GROUP), GROUP)
            student, teacher = logits[half, 0, at, :], logits[half, 1, at, :]
            inverse, shift = res_at[here, 0:1], res_at[here, 1:2]
            ratio = student * (1.0 / 30.0)
            value = (
                jnp.exp(student) * inverse * (student - teacher + shift) * (1.0 - ratio * ratio)
            ).astype(BF16)
            grads[half, x, at, :] = value

        for turn in (0, 1):
            for side, to in ((0, right), (1, left)):
                mine = grads.at[half, x, pl.ds(32 * ((side + turn) % 2), 32)]
                remote(mine, mine, g_ss.at[half, side, turn], g_rs.at[half, side, turn], at_x(to)).start()

    def forward(half):
        for side, chunk, to in ((0, left, right), (1, right, left)):
            src = grads.at[half, chunk, pl.ds(32 * side, 32)]
            landed(src, g_rs.at[half, side, 0])
            remote(src, src, f_ss.at[half, side], f_rs.at[half, side], at_x(to)).start()

    def gathered(half):
        landed(grads.at[half, left, pl.ds(32, 32)], g_rs.at[half, 0, 1])
        landed(grads.at[half, right, pl.ds(0, 32)], g_rs.at[half, 1, 1])
        landed(grads.at[half, across, pl.ds(0, 32)], f_rs.at[half, 0])
        landed(grads.at[half, across, pl.ds(32, 32)], f_rs.at[half, 1])

    def all_rows(half):
        return grads[half, :, :, 0:COLS].reshape(NX * ROWS, COLS)

    def hidden_product(half):
        rows = all_rows(half)
        for lo, hi in ((0, 256), (256, 512), (512, 768), (768, 896)):
            block = jnp.dot(rows, ws[:, lo:hi], preferred_element_type=F32)
            hp[half, :, :, :, :, lo:hi] = block.reshape(4, 4, 2, 8, hi - lo)
        remote(
            hp.at[half, :, :, 1 - c], hc.at[half], hc_ss.at[half], hc_rs.at[half], at_v(y, z, 1 - c)
        ).start()

    def weight_product(half):
        rows = ls[half].reshape(NX * ROWS, ls.shape[-1])

        @pl.loop(0, WIDE // 256)
        def _(i):
            at = pl.ds(pl.multiple_of(i * 256, 256), 256)
            lhs = grads[half, :, :, at].reshape(NX * ROWS, 256)
            block = lax.dot_general(lhs, rows, (((0,), (0,)), ((), ())), preferred_element_type=F32)
            if half == 0:
                wg_acc[at, :] = block
            else:
                wg_stage[at, :] = (wg_acc[at, :] + block).astype(BF16)

    def own_gradient():
        @pl.loop(0, WIDE // 128)
        def _(i):
            at = pl.ds(pl.multiple_of(i * 128, 128), 128)
            block = jnp.concatenate([grads[0, x, :, at], grads[1, x, :, at]], axis=0)
            grad_stage[at, :] = jnp.transpose(block.astype(F32)).astype(BF16)

    def hidden_y(half):
        landed(hc.at[half], hc_rs.at[half])
        for k in range(4):
            total = hp[half, k, :, c] + hc[half, k]
            ysum[half, k] = total.reshape(32, 896).astype(BF16)
        for step in (1, 3, 2):
            to = (y + step) % 4
            remote(
                ysum.at[half, to], yr.at[half, step], hy_ss.at[half, step], hy_rs.at[half, step],
                at_v(to, z, c),
            ).start()

    def hidden_z(half):
        total = ysum[half, y].astype(F32)
        for step in (1, 2, 3):
            landed(yr.at[half, step], hy_rs.at[half, step])
            total = total + yr[half, step].astype(F32)
        zs[half] = total.reshape(4, 8, 896).astype(BF16)
        for k in range(4):
            zz = 4 * half + k

            @pl.when(zz != z)
            def _():
                remote(
                    zs.at[half, k], zr.at[z], hz_ss.at[half, k], hz_rs.at[z], at_v(y, zz, c)
                ).start()

    def hidden_end(half):
        @pl.when(z // 4 == half)
        def _():
            zr[z] = zs[half, z % 4]
            for step in range(1, 8):
                who = (z + step) % 8
                landed(zr.at[who], hz_rs.at[who])
            total = zr[0].astype(F32)
            for k in range(1, 8):
                total = total + zr[k].astype(F32)
            hg_out[...] = total.astype(BF16)

    S, T = 0, 1
    for half in range(HALVES):
        z_arrive(S, hs, half)
        y_send(S, hs, half)
    y_arrive(S, hs, 0)
    c_send(S, hs, 0)
    for half in range(HALVES):
        z_arrive(T, ht, half)
        y_send(T, ht, half)
    c_arrive(S, hs, 0)
    layout(S, hs, ls, 0)
    load_s.wait()
    hop_one(S, 0)
    y_arrive(S, hs, 1)
    c_send(S, hs, 1)
    c_arrive(S, hs, 1)
    layout(S, hs, ls, 1)
    hop_one(S, 1)
    y_arrive(T, ht, 0)
    c_send(T, ht, 0)
    hop_two(S, 0)
    load_t.wait()
    c_arrive(T, ht, 0)
    layout(T, ht, lt, 0)
    hop_one(T, 0)
    y_arrive(T, ht, 1)
    c_send(T, ht, 1)
    c_arrive(T, ht, 1)
    layout(T, ht, lt, 1)
    hop_one(T, 1)
    hop_two(T, 0)
    hop_two(S, 1)
    hop_two(T, 1)
    finish(S, 0)
    finish(T, 0)
    stats_one(0)
    finish(S, 1)
    stats_two(0)
    gradient(0)
    finish(T, 1)
    stats_one(1)
    forward(0)
    stats_two(1)
    gradient(1)
    gathered(0)
    hidden_product(0)
    forward(1)
    hidden_y(0)
    weight_product(0)
    own_gradient()
    store_grad = pltpu.make_async_copy(grad_stage.at[pl.ds(0, COLS)], grad_out, out_sem.at[1])
    store_grad.start()
    hidden_z(0)
    gathered(1)
    hidden_product(1)
    hidden_y(1)
    weight_product(1)
    store = pltpu.make_async_copy(wg_stage.at[pl.ds(0, COLS)], wg_out, out_sem.at[0])
    store.start()
    hidden_z(1)
    lane = lax.broadcasted_iota(jnp.int32, (1, 128), 1)
    kl_out[...] = jnp.where(lane < ROWS, back[0, 0:1, :], back[1, 0:1, :])
    chosen_out[...] = jnp.where(lane < ROWS, back[0, 1:3, :], back[1, 1:3, :])
    hidden_end(0)
    hidden_end(1)
    store.wait()
    store_grad.wait()

    for m, ref in both:
        for step in range(1, 8):
            left_here(ref.at[y, z, c], zsnd.at[m, step])
        for half in range(HALVES):
            for step in (1, 2, 3):
                left_here(ref.at[y, pl.ds(4 * half, 4), c], ysnd.at[m, half, step])
            left_here(ref.at[:, pl.ds(4 * half, 4), c], csnd.at[m, half])
    for u in range(4):
        for side in (0, 1):
            left_here(one_s.at[u, pl.ds(0, 32)], one_ss.at[u, side])
            left_here(two_s.at[u, side], two_ss.at[u, side])
    for half in range(HALVES):
        for step in range(1, 8):
            left_here(sr1.at[half, group], s1_ss.at[half, step])
            left_here(sr2.at[half, z], s2_ss.at[half, step])
        for side in (0, 1):
            for turn in (0, 1):
                left_here(grads.at[half, x, pl.ds(0, 32)], g_ss.at[half, side, turn])
            left_here(grads.at[half, x, pl.ds(0, 32)], f_ss.at[half, side])
        left_here(hc.at[half], hc_ss.at[half])
        for step in (1, 2, 3):
            left_here(ysum.at[half, 0], hy_ss.at[half, step])
        for k in range(4):

            @pl.when(4 * half + k != z)
            def _():
                left_here(zs.at[half, k], hz_ss.at[half, k])


PIECES = tuple((lo, min(lo + 256, COLS)) for lo in range(0, COLS, 256))


def hand_on(kl, chosen, grad, wg, hg, kl_out, chosen_out, grad_out, wg_out, hg_out, wg_here, grad_here, sems):
    first, second = [], []
    for source, here, target, pieces in ((wg, wg_here, wg_out, PIECES), (grad, grad_here, grad_out, ((0, COLS),))):
        for lo, hi in pieces:
            i = len(first)
            first.append(pltpu.make_async_copy(source.at[lo:hi], here.at[lo:hi], sems.at[0, i]))
            second.append(pltpu.make_async_copy(here.at[lo:hi], target.at[lo:hi], sems.at[1, i]))
    for copy in first:
        copy.start()
    kl_out[...] = kl[...]
    chosen_out[...] = chosen[...]
    hg_out[...] = hg[...]
    for one, two in zip(first, second):
        one.wait()
        two.start()
    for copy in second:
        copy.wait()


def body(teacher_hidden, student_hidden, teacher_weight, student_weight, sampled_ids):
    dma, vmem = pltpu.SemaphoreType.DMA, pltpu.VMEM
    on_chip = pl.BlockSpec(memory_space=pltpu.VMEM)
    any_space = pl.BlockSpec(memory_space=pl.ANY)
    kt, ks = teacher_weight.shape[0], student_weight.shape[0]
    outs = (
        jax.ShapeDtypeStruct((1, 128), F32),
        jax.ShapeDtypeStruct((2, 128), F32),
        jax.ShapeDtypeStruct((COLS, 128), BF16),
        jax.ShapeDtypeStruct((COLS, ks), BF16),
        jax.ShapeDtypeStruct((8, ks), BF16),
    )
    results = pl.pallas_call(
        kernel,
        out_shape=outs,
        in_specs=[on_chip, on_chip, on_chip, any_space, any_space],
        out_specs=(on_chip, on_chip, any_space, any_space, on_chip),
        scratch_shapes=[
            vmem((COLS, kt), BF16), vmem((COLS, ks), BF16),
            vmem((4, 8, 2, 8, kt), BF16), vmem((4, 8, 2, 8, ks), BF16),
            vmem((2, 4, ROWS, kt), BF16), vmem((2, 4, ROWS, ks), BF16),
            vmem((3, ROWS, WIDE), F32),
            vmem((4, ROWS, WIDE), I16), vmem((4, 2, 32, WIDE), I16),
            vmem((4, 2, ROWS, WIDE), I16), vmem((4, 2, ROWS, WIDE), I16),
            vmem((2, 2, ROWS, WIDE), F32),
            vmem((128, 128), F32), vmem((128, 128), F32),
            vmem((2, 8, 8, 128), F32), vmem((2, 8, 8, 128), F32),
            vmem((128, 128), F32), vmem((128, 128), F32), vmem((2, 8, 128), F32),
            vmem((2, 4, ROWS, WIDE), BF16),
            vmem((WIDE, ks), F32), vmem((WIDE, ks), BF16), vmem((WIDE, 128), BF16),
            vmem((2, 4, 4, 2, 8, ks), F32), vmem((2, 4, 4, 8, ks), F32),
            vmem((2, 4, 32, ks), BF16), vmem((2, 4, 32, ks), BF16),
            vmem((2, 4, 8, ks), BF16), vmem((8, 8, ks), BF16),
            dma((2,)), dma((2, 8)), dma((2, 8)), dma((2, 2, 4)), dma((2, 2, 4)), dma((2, 2)), dma((2, 2)),
            dma((4, 2)), dma((4, 2)), dma((4, 2)), dma((4, 2)),
            dma((2, 8)), dma((2, 8)), dma((2, 8)), dma((2, 8)),
            dma((2, 2, 2)), dma((2, 2, 2)), dma((2, 2)), dma((2, 2)),
            dma((2,)), dma((2,)), dma((2, 4)), dma((2, 4)), dma((2, 4)), dma((8,)), dma((2,)),
        ],
        compiler_params=pltpu.CompilerParams(
            collective_id=0, has_side_effects=True, vmem_limit_bytes=60 * 1024 * 1024
        ),
    )(teacher_hidden, student_hidden, sampled_ids.reshape(1, 128), teacher_weight.T, student_weight.T)
    specs = (on_chip, on_chip, any_space, any_space, on_chip)
    kl, chosen, grad, weight_grad, hidden_grad = pl.pallas_call(
        hand_on,
        out_shape=outs,
        in_specs=specs,
        out_specs=specs,
        scratch_shapes=[vmem((COLS, ks), BF16), vmem((COLS, 128), BF16), dma((2, len(PIECES) + 1))],
        compiler_params=pltpu.CompilerParams(vmem_limit_bytes=60 * 1024 * 1024),
    )(*results)
    return kl.reshape(128), chosen, grad.T, weight_grad.T, hidden_grad


def solution(mesh):
    placed = (P("vocab", "row"), P("vocab", "row"), P("row", "vocab"), P("row", "vocab"), P("row"))
    return jax.shard_map(
        body,
        mesh=mesh,
        in_specs=placed,
        out_specs=(P("row"), P(None, "row"), P("row", "vocab"), P("row", "vocab"), P("vocab", "row")),
        check_vma=False,
    )
```

```python
import jax
import jax.numpy as jnp
from jax import lax
from jax.experimental import pallas as pl
from jax.experimental.pallas import tpu as pltpu
from jax.sharding import PartitionSpec as P

MESH = pl.DeviceIdType.MESH
F32, BF16, I16 = jnp.float32, jnp.bfloat16, jnp.int16
NX, NY, NZ, NC = 4, 4, 8, 2
OWN = 128
PARTS = ((0, 64), (64, 32), (96, 32))
COLS = 2000
WIDE = 2048
TAIL = WIDE - 128
GROUP = 16
SCALE = 32000.0
BLOCKS = ((0, 512), (512, 1024), (1024, 1536), (1536, COLS))


def softcap(values):
    return 30.0 * jnp.tanh(values * (1.0 / 30.0))


def encode(values, ref, at):
    most = jnp.max(jnp.abs(values), axis=1, keepdims=True)
    power = jnp.ceil(jnp.log2(jnp.maximum(most, 1e-30)))
    whole = jnp.round(values * (jnp.exp2(-power) * SCALE))
    lane = lax.broadcasted_iota(jnp.int32, (values.shape[0], 128), 1)
    last = jnp.where(lane >= COLS - TAIL, power, whole[:, TAIL:])
    ref[at, 0:TAIL] = whole[:, :TAIL].astype(I16)
    ref[at, TAIL:WIDE] = last.astype(I16)


def decode(ref, at):
    values = ref[at, :].astype(F32)
    lane = lax.broadcasted_iota(jnp.int32, (values.shape[0], 128), 1)
    power = jnp.max(jnp.where(lane >= COLS - TAIL, values[:, TAIL:], -1000.0), axis=1, keepdims=True)
    return values * (jnp.exp2(power) * (1.0 / SCALE))


def kernel(
    th, sh, ids, wt_hbm, ws_hbm,
    kl_out, chosen_out, grad_out, wg_out, hg_out,
    wt, ws, ht, hs, lt, ls, part, own_part, one_s, one_r, two_s, two_r, logits, stat, ids_at, sr1, sr2, res, res_at, back,
    grads, wg_acc, wg_stage, grad_stage, hb, yr, zs, zr,
    ids_here, w_sem, zsnd, zrcv, ysnd, yrcv, csnd, crcv,
    one_ss, one_rs, two_ss, two_rs, s1_ss, s1_rs, s2_ss, s2_rs, g_ss, g_rs, f_ss, f_rs,
    hy_ss, hy_rs, hz_ss, hz_rs, out_sem,
):
    x = lax.axis_index("row")
    v = lax.axis_index("vocab")
    y, z, c = v // 16, (v // 2) % 8, v % 2
    right, left, across = (x + 1) % 4, (x + 3) % 4, (x + 2) % 4

    def at_x(to):
        return (to, v)

    def at_v(ty, tz, tc):
        return (x, ty * 16 + tz * 2 + tc)

    def remote(src, dst, ss, rs, device):
        return pltpu.make_async_remote_copy(
            src_ref=src, dst_ref=dst, send_sem=ss, recv_sem=rs, device_id=device, device_id_type=MESH
        )

    def landed(ref, sem):
        remote(ref, ref, sem, sem, at_x(right)).wait_recv()

    def left_here(ref, sem):
        remote(ref, ref, sem, sem, at_x(right)).wait_send()

    barrier = pltpu.get_barrier_semaphore()
    for to in (right, left):
        pl.semaphore_signal(barrier, inc=1, device_id=at_x(to), device_id_type=MESH)
    for step in range(1, 8):
        pl.semaphore_signal(
            barrier, inc=1, device_id=at_v((y + step // 2) % 4, z, (c + step) % 2), device_id_type=MESH
        )
        pl.semaphore_signal(barrier, inc=1, device_id=at_v(y, (z + step) % 8, c), device_id_type=MESH)

    loads = [
        pltpu.make_async_copy(source, target, w_sem.at[i])
        for i, (source, target) in enumerate(
            ((sh, hs.at[y, z, c]), (th, ht.at[y, z, c]), (ids, ids_here), (ws_hbm, ws), (wt_hbm, wt))
        )
    ]
    for load in loads:
        load.start()
    part[:, :, TAIL:WIDE] = jnp.zeros((3, OWN, 128), F32)
    own_part[:, :, TAIL:WIDE] = jnp.zeros((2, OWN, 128), F32)
    stat[...] = jnp.zeros((128, 128), F32)
    res[...] = jnp.zeros((128, 128), F32)
    for load in loads[:3]:
        load.wait()
    ids_at[...] = jnp.transpose(jnp.broadcast_to(ids_here[...].astype(F32), (128, 128)))

    pl.semaphore_wait(barrier, 16)

    both = ((0, hs), (1, ht))
    for m, ref in both:
        for step in range(1, 8):
            to = (z + step) % 8
            remote(
                ref.at[y, z, c], ref.at[y, z, c], zsnd.at[m, step], zrcv.at[m, z], at_v(y, to, c)
            ).start()

    def block_rows(b):
        first, rows = PARTS[b]
        return first // 16, rows // 16

    def z_arrive(m, ref, b):
        first, count = block_rows(b)
        for zz in range(first, first + count):

            @pl.when(zz != z)
            def _():
                landed(ref.at[y, zz, c], zrcv.at[m, zz])

    def y_send(m, ref, b):
        src = ref.at[y, pl.ds(*block_rows(b)), c]
        for step in (1, 3, 2):
            remote(
                src, src, ysnd.at[m, b, step], yrcv.at[m, b, y], at_v((y + step) % 4, z, c)
            ).start()

    def y_arrive(m, ref, b):
        for step in (1, 3, 2):
            yy = (y + step) % 4
            landed(ref.at[yy, pl.ds(*block_rows(b)), c], yrcv.at[m, b, yy])

    def c_send(m, ref, b):
        src = ref.at[:, pl.ds(*block_rows(b)), c]
        remote(src, src, csnd.at[m, b], crcv.at[m, b], at_v(y, z, 1 - c)).start()

    def c_arrive(m, ref, b):
        first, count = block_rows(b)
        landed(ref.at[:, pl.ds(first, count), 1 - c], crcv.at[m, b])
        rows = (ls, lt)[m]
        for k in range(4):
            block = ref[k, first : first + count].astype(F32)
            rows[k, 16 * first : 16 * (first + count), :] = block.reshape(16 * count, rows.shape[-1]).astype(BF16)

    def product(m, b, chunks, targets):
        first, count = PARTS[b]
        rows, weight = (ls, ws) if m == 0 else (lt, wt)
        lhs = jnp.concatenate([rows[chunk, first : first + count, :] for chunk in chunks], axis=0)
        for lo, hi in BLOCKS:
            block = lax.dot_general(
                lhs, weight[lo:hi, :], (((1,), (1,)), ((), ())), preferred_element_type=F32
            )
            for i, target in enumerate(targets):
                target[first : first + count, lo:hi] = block[i * count : (i + 1) * count, :]

    def hop_one(m, b):
        first, count = PARTS[b]
        product(m, b, (across, x), (part.at[0], own_part.at[m]))

        @pl.loop(0, count // GROUP)
        def _(g):
            at = pl.ds(pl.multiple_of(first + g * GROUP, GROUP), GROUP)
            encode(part[0, at, :], one_s.at[m], at)

        some = count // 2
        for side, to in ((0, right), (1, left)):
            remote(
                one_s.at[m, pl.ds(first + side * some, some)], one_r.at[m, side, pl.ds(first // 2, some)],
                one_ss.at[m, b, side], one_rs.at[m, b, side], at_x(to),
            ).start()

    def hop_two(m, b):
        first, count = PARTS[b]
        some = count // 2
        product(m, b, (right, left), (part.at[1], part.at[2]))
        for side, to in ((0, right), (1, left)):
            landed(one_r.at[m, side, pl.ds(first // 2, some)], one_rs.at[m, b, side])

            @pl.loop(0, some // GROUP)
            def _(g):
                inner = pl.ds(pl.multiple_of(first // 2 + g * GROUP, GROUP), GROUP)
                at = pl.ds(pl.multiple_of(first + side * some + g * GROUP, GROUP), GROUP)
                plain = pl.ds(pl.multiple_of(first + (1 - side) * some + g * GROUP, GROUP), GROUP)
                encode(part[1 + side, at, :] + decode(one_r.at[m, side], inner), two_s.at[m, side], at)
                encode(part[1 + side, plain, :], two_s.at[m, side], plain)

            at = pl.ds(first, count)
            remote(
                two_s.at[m, side, at], two_r.at[m, side, at], two_ss.at[m, b, side], two_rs.at[m, b, side], at_x(to)
            ).start()

    def finish(m, b):
        first, count = PARTS[b]
        for side in (0, 1):
            landed(two_r.at[m, side, pl.ds(first, count)], two_rs.at[m, b, side])
        column = lax.broadcasted_iota(jnp.int32, (GROUP, WIDE), 1)
        lane = lax.broadcasted_iota(jnp.int32, (GROUP, 128), 1)

        @pl.loop(0, count // GROUP)
        def _(g):
            at = pl.ds(pl.multiple_of(first + g * GROUP, GROUP), GROUP)
            raw = own_part[m, at, :] + decode(two_r.at[m, 0], at) + decode(two_r.at[m, 1], at)
            capped = softcap(raw)
            logits[m, at, :] = capped
            if m == 1:
                student = logits[0, at, :]
                valid = column < COLS
                t_exp = jnp.where(valid, jnp.exp(capped), 0.0)
                s_exp = jnp.where(valid, jnp.exp(student), 0.0)
                wanted = ids_at[at, 0:1].astype(jnp.int32) - v * COLS
                hit = jnp.logical_and(column == wanted, valid)
                sums = (
                    t_exp,
                    jnp.where(hit, capped, 0.0),
                    s_exp,
                    s_exp * (student - capped),
                    jnp.where(hit, student, 0.0),
                )
                tile = jnp.zeros((GROUP, 128), F32)
                for j, term in enumerate(sums):
                    tile = jnp.where(lane == j, jnp.sum(term, axis=1, keepdims=True), tile)
                stat[at, :] = tile

    group = y * 2 + c

    def stats_one(half):
        sr1[half, group] = jnp.transpose(stat[...])[0:8, :]
        for step in range(1, 8):
            remote(
                sr1.at[half, group], sr1.at[half, group], s1_ss.at[half, step], s1_rs.at[half, group],
                at_v((y + step // 2) % 4, z, (c + step) % 2),
            ).start()

    def stats_two(half):
        for step in range(1, 8):
            who = ((y + step // 2) % 4) * 2 + (c + step) % 2
            landed(sr1.at[half, who], s1_rs.at[half, who])
        total = sr1[half, 0]
        for k in range(1, 8):
            total = total + sr1[half, k]
        sr2[half, z] = total
        for step in range(1, 8):
            remote(
                sr2.at[half, z], sr2.at[half, z], s2_ss.at[half, step], s2_rs.at[half, z],
                at_v(y, (z + step) % 8, c),
            ).start()

    def gradient(half):
        for step in range(1, 8):
            who = (z + step) % 8
            landed(sr2.at[half, who], s2_rs.at[half, who])
        total = sr2[half, 0]
        for k in range(1, 8):
            total = total + sr2[half, k]
        t_total, t_pick, s_total, cross, s_pick = (total[j : j + 1, :] for j in range(5))
        s_log, t_log = jnp.log(s_total), jnp.log(t_total)
        divergence = cross / s_total - s_log + t_log
        res[0:1, :] = 1.0 / s_total
        res[1:2, :] = t_log - s_log - divergence
        back[half, 0:1, :] = divergence
        back[half, 1:2, :] = s_pick - s_log
        back[half, 2:3, :] = t_pick - t_log
        res_at[...] = jnp.transpose(res[...])

        first, count = PARTS[half]

        @pl.loop(0, count // GROUP)
        def _(g):
            at = pl.ds(pl.multiple_of(first + g * GROUP, GROUP), GROUP)
            student, teacher = logits[0, at, :], logits[1, at, :]
            inverse, shift = res_at[at, 0:1], res_at[at, 1:2]
            ratio = student * (1.0 / 30.0)
            grads[x, at, :] = (
                jnp.exp(student) * inverse * (student - teacher + shift) * (1.0 - ratio * ratio)
            ).astype(BF16)

        some = count // 2
        for turn in (0, 1):
            for side, to in ((0, right), (1, left)):
                mine = grads.at[x, pl.ds(first + some * ((side + turn) % 2), some)]
                remote(mine, mine, g_ss.at[half, side, turn], g_rs.at[half, side, turn], at_x(to)).start()

    def forward(b):
        first, count = PARTS[b]
        some = count // 2
        for side, chunk, to in ((0, left, right), (1, right, left)):
            src = grads.at[chunk, pl.ds(first + some * side, some)]
            landed(src, g_rs.at[b, side, 0])
            remote(src, src, f_ss.at[b, side], f_rs.at[b, side], at_x(to)).start()

    def gathered(b):
        first, count = PARTS[b]
        some = count // 2
        landed(grads.at[left, pl.ds(first + some, some)], g_rs.at[b, 0, 1])
        landed(grads.at[right, pl.ds(first, some)], g_rs.at[b, 1, 1])
        landed(grads.at[across, pl.ds(first, some)], f_rs.at[b, 0])
        landed(grads.at[across, pl.ds(first + some, some)], f_rs.at[b, 1])

    def hidden_product(b):
        first, count = PARTS[b]
        rows = grads[:, first : first + count, 0:COLS].reshape(NX * count, COLS)
        at = slice(first // 2, (first + count) // 2)
        for lo, hi in ((0, 256), (256, 512), (512, 768), (768, 896)):
            block = jnp.dot(rows, ws[:, lo:hi], preferred_element_type=F32)
            block = block.reshape(4, count // 16, 2, 8, hi - lo)
            for k in range(4):
                for core in range(2):
                    hb[k, core, at, lo:hi] = block[k, :, core].reshape(count // 2, hi - lo).astype(BF16)
        at = pl.ds(first // 2, count // 2)
        for step in range(1, 8):
            ty, tc = (y + step // 2) % 4, (c + step) % 2
            remote(
                hb.at[ty, tc, at], yr.at[group, at], hy_ss.at[b, step], hy_rs.at[b, group], at_v(ty, z, tc)
            ).start()

    def weight_product(half):
        rows = ls[:, half * 64 : half * 64 + 64, :].reshape(NX * 64, ls.shape[-1])

        @pl.loop(0, WIDE // 256)
        def _(i):
            at = pl.ds(pl.multiple_of(i * 256, 256), 256)
            lhs = grads[:, half * 64 : half * 64 + 64, at].reshape(NX * 64, 256)
            block = lax.dot_general(lhs, rows, (((0,), (0,)), ((), ())), preferred_element_type=F32)
            if half == 0:
                wg_acc[at, :] = block
            else:
                wg_stage[at, :] = (wg_acc[at, :] + block).astype(BF16)

    def own_gradient():
        @pl.loop(0, WIDE // 128)
        def _(i):
            at = pl.ds(pl.multiple_of(i * 128, 128), 128)
            grad_stage[at, :] = jnp.transpose(grads[x, :, at].astype(F32)).astype(BF16)

    def hidden_z(b):
        first, count = block_rows(b)
        at = pl.ds(8 * first, 8 * count)
        total = hb[y, c, 8 * first : 8 * (first + count), :].astype(F32)
        for step in range(1, 8):
            who = ((y + step // 2) % 4) * 2 + (c + step) % 2
            landed(yr.at[who, at], hy_rs.at[b, who])
            total = total + yr[who, 8 * first : 8 * (first + count), :].astype(F32)
        zs[first : first + count] = total.reshape(count, 8, 896).astype(BF16)
        for zz in range(first, first + count):

            @pl.when(zz != z)
            def _():
                remote(zs.at[zz], zr.at[z], hz_ss.at[zz], hz_rs.at[z], at_v(y, zz, c)).start()

    def hidden_end():
        zr[z] = zs[z]
        for step in range(1, 8):
            who = (z + step) % 8
            landed(zr.at[who], hz_rs.at[who])
        total = zr[0].astype(F32)
        for k in range(1, 8):
            total = total + zr[k].astype(F32)
        hg_out[...] = total.astype(BF16)

    S, T = 0, 1
    for b in range(3):
        z_arrive(S, hs, b)
        y_send(S, hs, b)
    y_arrive(S, hs, 0)
    c_send(S, hs, 0)
    for b in range(3):
        z_arrive(T, ht, b)
        y_send(T, ht, b)
    c_arrive(S, hs, 0)
    loads[3].wait()
    hop_one(S, 0)
    for b in (1, 2):
        y_arrive(S, hs, b)
        c_send(S, hs, b)
    for b in (1, 2):
        c_arrive(S, hs, b)
        hop_one(S, b)
    y_arrive(T, ht, 0)
    c_send(T, ht, 0)
    hop_two(S, 0)
    loads[4].wait()
    c_arrive(T, ht, 0)
    hop_one(T, 0)
    for b in (1, 2):
        y_arrive(T, ht, b)
        c_send(T, ht, b)
    hop_two(S, 1)
    hop_two(T, 0)
    for b in (1, 2):
        c_arrive(T, ht, b)
        hop_one(T, b)
    finish(S, 0)
    hop_two(S, 2)
    finish(T, 0)
    stats_one(0)
    hop_two(T, 1)
    hop_two(T, 2)
    finish(S, 1)
    stats_two(0)
    finish(T, 1)
    stats_one(1)
    finish(S, 2)
    gradient(0)
    stats_two(1)
    finish(T, 2)
    stats_one(2)
    gradient(1)
    forward(0)
    stats_two(2)
    forward(1)
    gradient(2)
    gathered(0)
    hidden_product(0)
    forward(2)
    gathered(1)
    hidden_product(1)
    own_gradient()
    store_grad = pltpu.make_async_copy(grad_stage.at[pl.ds(0, COLS)], grad_out, out_sem.at[1])
    store_grad.start()
    hidden_z(0)
    weight_product(0)
    gathered(2)
    hidden_product(2)
    hidden_z(1)
    weight_product(1)
    store = pltpu.make_async_copy(wg_stage.at[pl.ds(0, COLS)], wg_out, out_sem.at[0])
    store.start()
    hidden_z(2)
    lane = lax.broadcasted_iota(jnp.int32, (1, 128), 1)
    final = back[0]
    for b in (1, 2):
        final = jnp.where(lane < PARTS[b][0], final, back[b])
    kl_out[...] = final[0:1, :]
    chosen_out[...] = final[1:3, :]
    hidden_end()
    store.wait()
    store_grad.wait()

    for m, ref in both:
        for step in range(1, 8):
            left_here(ref.at[y, z, c], zsnd.at[m, step])
        for b in range(3):
            for step in (1, 2, 3):
                left_here(ref.at[y, pl.ds(*block_rows(b)), c], ysnd.at[m, b, step])
            left_here(ref.at[:, pl.ds(*block_rows(b)), c], csnd.at[m, b])
    for m in (0, 1):
        for b, (first, count) in enumerate(PARTS):
            for side in (0, 1):
                left_here(one_s.at[m, pl.ds(first, count // 2)], one_ss.at[m, b, side])
                left_here(two_s.at[m, side, pl.ds(first, count)], two_ss.at[m, b, side])
    for b, (first, count) in enumerate(PARTS):
        for step in range(1, 8):
            left_here(sr1.at[b, group], s1_ss.at[b, step])
            left_here(sr2.at[b, z], s2_ss.at[b, step])
            left_here(hb.at[y, c, pl.ds(first // 2, count // 2)], hy_ss.at[b, step])
        for side in (0, 1):
            left_here(grads.at[x, pl.ds(first, count // 2)], f_ss.at[b, side])
            for turn in (0, 1):
                left_here(grads.at[x, pl.ds(first, count // 2)], g_ss.at[b, side, turn])
    for zz in range(8):

        @pl.when(zz != z)
        def _():
            left_here(zs.at[zz], hz_ss.at[zz])


PIECES = tuple((lo, min(lo + 256, COLS)) for lo in range(0, COLS, 256))


def hand_on(*refs):
    sources, targets, here, sems = refs[:5], refs[5:10], refs[10:15], refs[15]
    first, second = [], []
    for k, (source, target, stage) in enumerate(zip(sources, targets, here)):
        for lo, hi in PIECES if k == 3 else ((0, source.shape[0]),):
            i = len(first)
            first.append(pltpu.make_async_copy(source.at[lo:hi], stage.at[lo:hi], sems.at[0, i]))
            second.append(pltpu.make_async_copy(stage.at[lo:hi], target.at[lo:hi], sems.at[1, i]))
    for copy in first:
        copy.start()
    for one, two in zip(first, second):
        one.wait()
        two.start()
    for copy in second:
        copy.wait()


def body(teacher_hidden, student_hidden, teacher_weight, student_weight, sampled_ids):
    dma, vmem = pltpu.SemaphoreType.DMA, pltpu.VMEM
    on_chip = pl.BlockSpec(memory_space=pltpu.VMEM)
    any_space = pl.BlockSpec(memory_space=pl.ANY)
    kt, ks = teacher_weight.shape[0], student_weight.shape[0]
    outs = (
        jax.ShapeDtypeStruct((1, 128), F32),
        jax.ShapeDtypeStruct((2, 128), F32),
        jax.ShapeDtypeStruct((COLS, 128), BF16),
        jax.ShapeDtypeStruct((COLS, ks), BF16),
        jax.ShapeDtypeStruct((8, ks), BF16),
    )
    results = pl.pallas_call(
        kernel,
        out_shape=outs,
        in_specs=[any_space] * 5,
        out_specs=(on_chip, on_chip, any_space, any_space, on_chip),
        scratch_shapes=[
            vmem((COLS, kt), BF16), vmem((COLS, ks), BF16),
            vmem((4, 8, 2, 8, kt), BF16), vmem((4, 8, 2, 8, ks), BF16),
            vmem((4, OWN, kt), BF16), vmem((4, OWN, ks), BF16),
            vmem((3, OWN, WIDE), F32), vmem((2, OWN, WIDE), F32),
            vmem((2, OWN, WIDE), I16), vmem((2, 2, OWN // 2, WIDE), I16),
            vmem((2, 2, OWN, WIDE), I16), vmem((2, 2, OWN, WIDE), I16),
            vmem((2, OWN, WIDE), F32),
            vmem((128, 128), F32), vmem((128, 128), F32),
            vmem((3, 8, 8, 128), F32), vmem((3, 8, 8, 128), F32),
            vmem((128, 128), F32), vmem((128, 128), F32), vmem((3, 8, 128), F32),
            vmem((4, OWN, WIDE), BF16),
            vmem((WIDE, ks), F32), vmem((WIDE, ks), BF16), vmem((WIDE, 128), BF16),
            vmem((4, 2, OWN // 2, ks), BF16), vmem((8, OWN // 2, ks), BF16),
            vmem((8, 8, ks), BF16), vmem((8, 8, ks), BF16), vmem((1, 128), jnp.int32),
            dma((5,)), dma((2, 8)), dma((2, 8)), dma((2, 3, 4)), dma((2, 3, 4)), dma((2, 3)), dma((2, 3)),
            dma((2, 3, 2)), dma((2, 3, 2)), dma((2, 3, 2)), dma((2, 3, 2)),
            dma((3, 8)), dma((3, 8)), dma((3, 8)), dma((3, 8)),
            dma((3, 2, 2)), dma((3, 2, 2)), dma((3, 2)), dma((3, 2)),
            dma((3, 8)), dma((3, 8)), dma((8,)), dma((8,)), dma((2,)),
        ],
        compiler_params=pltpu.CompilerParams(
            collective_id=0, has_side_effects=True, vmem_limit_bytes=60 * 1024 * 1024
        ),
    )(teacher_hidden, student_hidden, sampled_ids.reshape(1, 128), teacher_weight.T, student_weight.T)
    kl, chosen, grad, weight_grad, hidden_grad = pl.pallas_call(
        hand_on,
        out_shape=outs,
        in_specs=[any_space] * 5,
        out_specs=[any_space] * 5,
        scratch_shapes=[vmem(out.shape, out.dtype) for out in outs] + [dma((2, len(PIECES) + 4))],
        compiler_params=pltpu.CompilerParams(vmem_limit_bytes=60 * 1024 * 1024),
    )(*results)
    return kl.reshape(128), chosen, grad.T, weight_grad.T, hidden_grad


def solution(mesh):
    placed = (P("vocab", "row"), P("vocab", "row"), P("row", "vocab"), P("row", "vocab"), P("row"))
    return jax.shard_map(
        body,
        mesh=mesh,
        in_specs=placed,
        out_specs=(P("row"), P(None, "row"), P("row", "vocab"), P("row", "vocab"), P("vocab", "row")),
        check_vma=False,
    )
```

```python
import jax
import jax.numpy as jnp
from jax import lax
from jax.experimental import pallas as pl
from jax.experimental.pallas import tpu as pltpu
from jax.sharding import PartitionSpec as P

MESH = pl.DeviceIdType.MESH
F32, BF16, I16 = jnp.float32, jnp.bfloat16, jnp.int16
NX, NY, NZ, NC = 4, 4, 8, 2
OWN = 128
PARTS = ((0, 64), (64, 32), (96, 32))
COLS = 2000
WIDE = 2048
TAIL = WIDE - 128
GROUP = 16
FAR_FIRST = (4, 3, 5, 2, 6, 1, 7)
SCALE = 32000.0
BLOCKS = ((0, 512), (512, 1024), (1024, 1536), (1536, COLS))


def softcap(values):
    return 30.0 * jnp.tanh(values * (1.0 / 30.0))


def encode(values, ref, at):
    most = jnp.max(jnp.abs(values), axis=1, keepdims=True)
    power = jnp.ceil(jnp.log2(jnp.maximum(most, 1e-30)))
    whole = jnp.round(values * (jnp.exp2(-power) * SCALE))
    lane = lax.broadcasted_iota(jnp.int32, (values.shape[0], 128), 1)
    last = jnp.where(lane >= COLS - TAIL, power, whole[:, TAIL:])
    ref[at, 0:TAIL] = whole[:, :TAIL].astype(I16)
    ref[at, TAIL:WIDE] = last.astype(I16)


def decode(ref, at):
    values = ref[at, :].astype(F32)
    lane = lax.broadcasted_iota(jnp.int32, (values.shape[0], 128), 1)
    power = jnp.max(jnp.where(lane >= COLS - TAIL, values[:, TAIL:], -1000.0), axis=1, keepdims=True)
    return values * (jnp.exp2(power) * (1.0 / SCALE))


def kernel(
    th, sh, ids, wt_hbm, ws_hbm,
    kl_out, chosen_out, grad_out, wg_out, hg_out,
    wt, ws, ht, hs, lt, ls, part, own_part, one_s, one_r, two_s, two_r, logits, stat, ids_at, sr1, sr2, res, res_at, back,
    grads, wg_acc, wg_stage, grad_stage, hb, yr, zs, zr,
    ids_here, w_sem, zsnd, zrcv, ysnd, yrcv, csnd, crcv,
    one_ss, one_rs, two_ss, two_rs, s1_ss, s1_rs, s2_ss, s2_rs, g_ss, g_rs, f_ss, f_rs,
    hy_ss, hy_rs, hz_ss, hz_rs, out_sem,
):
    x = lax.axis_index("row")
    v = lax.axis_index("vocab")
    y, z, c = v // 16, (v // 2) % 8, v % 2
    right, left, across = (x + 1) % 4, (x + 3) % 4, (x + 2) % 4

    def at_x(to):
        return (to, v)

    def at_v(ty, tz, tc):
        return (x, ty * 16 + tz * 2 + tc)

    def remote(src, dst, ss, rs, device):
        return pltpu.make_async_remote_copy(
            src_ref=src, dst_ref=dst, send_sem=ss, recv_sem=rs, device_id=device, device_id_type=MESH
        )

    def landed(ref, sem):
        remote(ref, ref, sem, sem, at_x(right)).wait_recv()

    def left_here(ref, sem):
        remote(ref, ref, sem, sem, at_x(right)).wait_send()

    barrier = pltpu.get_barrier_semaphore()
    for to in (right, left):
        pl.semaphore_signal(barrier, inc=1, device_id=at_x(to), device_id_type=MESH)
    for step in FAR_FIRST:
        pl.semaphore_signal(
            barrier, inc=1, device_id=at_v((y + step // 2) % 4, z, (c + step) % 2), device_id_type=MESH
        )
        pl.semaphore_signal(barrier, inc=1, device_id=at_v(y, (z + step) % 8, c), device_id_type=MESH)

    loads = [
        pltpu.make_async_copy(source, target, w_sem.at[i])
        for i, (source, target) in enumerate(
            ((sh, hs.at[y, z, c]), (th, ht.at[y, z, c]), (ids, ids_here), (ws_hbm, ws), (wt_hbm, wt))
        )
    ]
    for load in loads:
        load.start()
    part[:, :, TAIL:WIDE] = jnp.zeros((3, OWN, 128), F32)
    own_part[:, :, TAIL:WIDE] = jnp.zeros((2, OWN, 128), F32)
    stat[...] = jnp.zeros((128, 128), F32)
    res[...] = jnp.zeros((128, 128), F32)
    for load in loads[:3]:
        load.wait()
    ids_at[...] = jnp.transpose(jnp.broadcast_to(ids_here[...].astype(F32), (128, 128)))

    pl.semaphore_wait(barrier, 16)

    both = ((0, hs), (1, ht))
    def z_send(m, ref):
        for step in FAR_FIRST:
            to = (z + step) % 8
            remote(
                ref.at[y, z, c], ref.at[y, z, c], zsnd.at[m, step], zrcv.at[m, z], at_v(y, to, c)
            ).start()

    z_send(0, hs)

    def block_rows(b):
        first, rows = PARTS[b]
        return first // 16, rows // 16

    def z_arrive(m, ref, b):
        first, count = block_rows(b)
        for zz in range(first, first + count):

            @pl.when(zz != z)
            def _():
                landed(ref.at[y, zz, c], zrcv.at[m, zz])

    def y_send(m, ref, b):
        src = ref.at[y, pl.ds(*block_rows(b)), c]
        for step in (1, 3, 2):
            remote(
                src, src, ysnd.at[m, b, step], yrcv.at[m, b, y], at_v((y + step) % 4, z, c)
            ).start()

    def y_arrive(m, ref, b):
        for step in (1, 3, 2):
            yy = (y + step) % 4
            landed(ref.at[yy, pl.ds(*block_rows(b)), c], yrcv.at[m, b, yy])

    def c_send(m, ref, b):
        src = ref.at[:, pl.ds(*block_rows(b)), c]
        remote(src, src, csnd.at[m, b], crcv.at[m, b], at_v(y, z, 1 - c)).start()

    def c_arrive(m, ref, b):
        first, count = block_rows(b)
        landed(ref.at[:, pl.ds(first, count), 1 - c], crcv.at[m, b])
        rows = (ls, lt)[m]
        for k in range(4):
            block = ref[k, first : first + count].astype(F32)
            rows[k, 16 * first : 16 * (first + count), :] = block.reshape(16 * count, rows.shape[-1]).astype(BF16)

    def product(m, b, chunks, targets):
        first, count = PARTS[b]
        rows, weight = (ls, ws) if m == 0 else (lt, wt)
        lhs = jnp.concatenate([rows[chunk, first : first + count, :] for chunk in chunks], axis=0)
        for lo, hi in BLOCKS:
            block = lax.dot_general(
                lhs, weight[lo:hi, :], (((1,), (1,)), ((), ())), preferred_element_type=F32
            )
            for i, target in enumerate(targets):
                target[first : first + count, lo:hi] = block[i * count : (i + 1) * count, :]

    def hop_one(m, b):
        first, count = PARTS[b]
        product(m, b, (across, x), (part.at[0], own_part.at[m]))

        @pl.loop(0, count // GROUP)
        def _(g):
            at = pl.ds(pl.multiple_of(first + g * GROUP, GROUP), GROUP)
            encode(part[0, at, :], one_s.at[m], at)

        some = count // 2
        for side, to in ((0, right), (1, left)):
            remote(
                one_s.at[m, pl.ds(first + side * some, some)], one_r.at[m, side, pl.ds(first // 2, some)],
                one_ss.at[m, b, side], one_rs.at[m, b, side], at_x(to),
            ).start()

    def hop_two(m, b):
        first, count = PARTS[b]
        some = count // 2
        product(m, b, (right, left), (part.at[1], part.at[2]))
        for side, to in ((0, right), (1, left)):
            landed(one_r.at[m, side, pl.ds(first // 2, some)], one_rs.at[m, b, side])

            @pl.loop(0, some // GROUP)
            def _(g):
                inner = pl.ds(pl.multiple_of(first // 2 + g * GROUP, GROUP), GROUP)
                at = pl.ds(pl.multiple_of(first + side * some + g * GROUP, GROUP), GROUP)
                plain = pl.ds(pl.multiple_of(first + (1 - side) * some + g * GROUP, GROUP), GROUP)
                encode(part[1 + side, at, :] + decode(one_r.at[m, side], inner), two_s.at[m, side], at)
                encode(part[1 + side, plain, :], two_s.at[m, side], plain)

            at = pl.ds(first, count)
            remote(
                two_s.at[m, side, at], two_r.at[m, side, at], two_ss.at[m, b, side], two_rs.at[m, b, side], at_x(to)
            ).start()

    def finish(m, b):
        first, count = PARTS[b]
        for side in (0, 1):
            landed(two_r.at[m, side, pl.ds(first, count)], two_rs.at[m, b, side])
        column = lax.broadcasted_iota(jnp.int32, (GROUP, WIDE), 1)
        lane = lax.broadcasted_iota(jnp.int32, (GROUP, 128), 1)

        @pl.loop(0, count // GROUP)
        def _(g):
            at = pl.ds(pl.multiple_of(first + g * GROUP, GROUP), GROUP)
            raw = own_part[m, at, :] + decode(two_r.at[m, 0], at) + decode(two_r.at[m, 1], at)
            capped = softcap(raw)
            logits[m, at, :] = capped
            if m == 1:
                student = logits[0, at, :]
                valid = column < COLS
                t_exp = jnp.where(valid, jnp.exp(capped), 0.0)
                s_exp = jnp.where(valid, jnp.exp(student), 0.0)
                wanted = ids_at[at, 0:1].astype(jnp.int32) - v * COLS
                hit = jnp.logical_and(column == wanted, valid)
                sums = (
                    t_exp,
                    jnp.where(hit, capped, 0.0),
                    s_exp,
                    s_exp * (student - capped),
                    jnp.where(hit, student, 0.0),
                )
                tile = jnp.zeros((GROUP, 128), F32)
                for j, term in enumerate(sums):
                    tile = jnp.where(lane == j, jnp.sum(term, axis=1, keepdims=True), tile)
                stat[at, :] = tile

    group = y * 2 + c

    def stats_one(half):
        sr1[half, group] = jnp.transpose(stat[...])[0:8, :]
        for step in FAR_FIRST:
            remote(
                sr1.at[half, group], sr1.at[half, group], s1_ss.at[half, step], s1_rs.at[half, group],
                at_v((y + step // 2) % 4, z, (c + step) % 2),
            ).start()

    def stats_two(half):
        for step in range(1, 8):
            who = ((y + step // 2) % 4) * 2 + (c + step) % 2
            landed(sr1.at[half, who], s1_rs.at[half, who])
        total = sr1[half, 0]
        for k in range(1, 8):
            total = total + sr1[half, k]
        sr2[half, z] = total
        for step in FAR_FIRST:
            remote(
                sr2.at[half, z], sr2.at[half, z], s2_ss.at[half, step], s2_rs.at[half, z],
                at_v(y, (z + step) % 8, c),
            ).start()

    def gradient(half):
        for step in range(1, 8):
            who = (z + step) % 8
            landed(sr2.at[half, who], s2_rs.at[half, who])
        total = sr2[half, 0]
        for k in range(1, 8):
            total = total + sr2[half, k]
        t_total, t_pick, s_total, cross, s_pick = (total[j : j + 1, :] for j in range(5))
        s_log, t_log = jnp.log(s_total), jnp.log(t_total)
        divergence = cross / s_total - s_log + t_log
        res[0:1, :] = 1.0 / s_total
        res[1:2, :] = t_log - s_log - divergence
        back[half, 0:1, :] = divergence
        back[half, 1:2, :] = s_pick - s_log
        back[half, 2:3, :] = t_pick - t_log
        res_at[...] = jnp.transpose(res[...])

        first, count = PARTS[half]

        @pl.loop(0, count // GROUP)
        def _(g):
            at = pl.ds(pl.multiple_of(first + g * GROUP, GROUP), GROUP)
            student, teacher = logits[0, at, :], logits[1, at, :]
            inverse, shift = res_at[at, 0:1], res_at[at, 1:2]
            ratio = student * (1.0 / 30.0)
            grads[x, at, :] = (
                jnp.exp(student) * inverse * (student - teacher + shift) * (1.0 - ratio * ratio)
            ).astype(BF16)

        some = count // 2
        for turn in (0, 1):
            for side, to in ((0, right), (1, left)):
                mine = grads.at[x, pl.ds(first + some * ((side + turn) % 2), some)]
                remote(mine, mine, g_ss.at[half, side, turn], g_rs.at[half, side, turn], at_x(to)).start()

    def forward(b):
        first, count = PARTS[b]
        some = count // 2
        for side, chunk, to in ((0, left, right), (1, right, left)):
            src = grads.at[chunk, pl.ds(first + some * side, some)]
            landed(src, g_rs.at[b, side, 0])
            remote(src, src, f_ss.at[b, side], f_rs.at[b, side], at_x(to)).start()

    def gathered(b):
        first, count = PARTS[b]
        some = count // 2
        landed(grads.at[left, pl.ds(first + some, some)], g_rs.at[b, 0, 1])
        landed(grads.at[right, pl.ds(first, some)], g_rs.at[b, 1, 1])
        landed(grads.at[across, pl.ds(first, some)], f_rs.at[b, 0])
        landed(grads.at[across, pl.ds(first + some, some)], f_rs.at[b, 1])

    def hidden_product(b):
        first, count = PARTS[b]
        rows = grads[:, first : first + count, 0:COLS].reshape(NX * count, COLS)
        at = slice(first // 2, (first + count) // 2)
        for lo, hi in ((0, 256), (256, 512), (512, 768), (768, 896)):
            block = jnp.dot(rows, ws[:, lo:hi], preferred_element_type=F32)
            block = block.reshape(4, count // 16, 2, 8, hi - lo)
            for k in range(4):
                for core in range(2):
                    hb[k, core, at, lo:hi] = block[k, :, core].reshape(count // 2, hi - lo).astype(BF16)
        at = pl.ds(first // 2, count // 2)
        for step in range(1, 8):
            ty, tc = (y + step // 2) % 4, (c + step) % 2
            remote(
                hb.at[ty, tc, at], yr.at[group, at], hy_ss.at[b, step], hy_rs.at[b, group], at_v(ty, z, tc)
            ).start()

    def weight_product(half):
        rows = ls[:, half * 64 : half * 64 + 64, :].reshape(NX * 64, ls.shape[-1])

        @pl.loop(0, WIDE // 256)
        def _(i):
            at = pl.ds(pl.multiple_of(i * 256, 256), 256)
            lhs = grads[:, half * 64 : half * 64 + 64, at].reshape(NX * 64, 256)
            block = lax.dot_general(lhs, rows, (((0,), (0,)), ((), ())), preferred_element_type=F32)
            if half == 0:
                wg_acc[at, :] = block
            else:
                wg_stage[at, :] = (wg_acc[at, :] + block).astype(BF16)

    def own_gradient():
        @pl.loop(0, WIDE // 128)
        def _(i):
            at = pl.ds(pl.multiple_of(i * 128, 128), 128)
            grad_stage[at, :] = jnp.transpose(grads[x, :, at].astype(F32)).astype(BF16)

    def hidden_z(b):
        first, count = block_rows(b)
        at = pl.ds(8 * first, 8 * count)
        total = hb[y, c, 8 * first : 8 * (first + count), :].astype(F32)
        for step in range(1, 8):
            who = ((y + step // 2) % 4) * 2 + (c + step) % 2
            landed(yr.at[who, at], hy_rs.at[b, who])
            total = total + yr[who, 8 * first : 8 * (first + count), :].astype(F32)
        zs[first : first + count] = total.reshape(count, 8, 896).astype(BF16)
        for zz in range(first, first + count):

            @pl.when(zz != z)
            def _():
                remote(zs.at[zz], zr.at[z], hz_ss.at[zz], hz_rs.at[z], at_v(y, zz, c)).start()

    def hidden_end():
        zr[z] = zs[z]
        for step in range(1, 8):
            who = (z + step) % 8
            landed(zr.at[who], hz_rs.at[who])
        total = zr[0].astype(F32)
        for k in range(1, 8):
            total = total + zr[k].astype(F32)
        hg_out[...] = total.astype(BF16)

    S, T = 0, 1
    z_arrive(S, hs, 0)
    y_send(S, hs, 0)
    z_send(T, ht)
    for b in (1, 2):
        z_arrive(S, hs, b)
        y_send(S, hs, b)
    y_arrive(S, hs, 0)
    c_send(S, hs, 0)
    for b in range(3):
        z_arrive(T, ht, b)
        y_send(T, ht, b)
    c_arrive(S, hs, 0)
    loads[3].wait()
    hop_one(S, 0)
    for b in (1, 2):
        y_arrive(S, hs, b)
        c_send(S, hs, b)
    for b in (1, 2):
        c_arrive(S, hs, b)
        hop_one(S, b)
    y_arrive(T, ht, 0)
    c_send(T, ht, 0)
    hop_two(S, 0)
    loads[4].wait()
    c_arrive(T, ht, 0)
    hop_one(T, 0)
    for b in (1, 2):
        y_arrive(T, ht, b)
        c_send(T, ht, b)
    hop_two(S, 1)
    hop_two(T, 0)
    for b in (1, 2):
        c_arrive(T, ht, b)
        hop_one(T, b)
    finish(S, 0)
    hop_two(S, 2)
    finish(T, 0)
    stats_one(0)
    hop_two(T, 1)
    hop_two(T, 2)
    finish(S, 1)
    stats_two(0)
    finish(T, 1)
    stats_one(1)
    finish(S, 2)
    gradient(0)
    stats_two(1)
    finish(T, 2)
    stats_one(2)
    forward(0)
    gradient(1)
    stats_two(2)
    forward(1)
    gradient(2)
    gathered(0)
    hidden_product(0)
    forward(2)
    gathered(1)
    hidden_product(1)
    own_gradient()
    store_grad = pltpu.make_async_copy(grad_stage.at[pl.ds(0, COLS)], grad_out, out_sem.at[1])
    store_grad.start()
    hidden_z(0)
    weight_product(0)
    gathered(2)
    hidden_product(2)
    hidden_z(1)
    weight_product(1)
    store = pltpu.make_async_copy(wg_stage.at[pl.ds(0, COLS)], wg_out, out_sem.at[0])
    store.start()
    hidden_z(2)
    lane = lax.broadcasted_iota(jnp.int32, (1, 128), 1)
    final = back[0]
    for b in (1, 2):
        final = jnp.where(lane < PARTS[b][0], final, back[b])
    kl_out[...] = final[0:1, :]
    chosen_out[...] = final[1:3, :]
    hidden_end()
    store.wait()
    store_grad.wait()

    for m, ref in both:
        for step in range(1, 8):
            left_here(ref.at[y, z, c], zsnd.at[m, step])
        for b in range(3):
            for step in (1, 2, 3):
                left_here(ref.at[y, pl.ds(*block_rows(b)), c], ysnd.at[m, b, step])
            left_here(ref.at[:, pl.ds(*block_rows(b)), c], csnd.at[m, b])
    for m in (0, 1):
        for b, (first, count) in enumerate(PARTS):
            for side in (0, 1):
                left_here(one_s.at[m, pl.ds(first, count // 2)], one_ss.at[m, b, side])
                left_here(two_s.at[m, side, pl.ds(first, count)], two_ss.at[m, b, side])
    for b, (first, count) in enumerate(PARTS):
        for step in range(1, 8):
            left_here(sr1.at[b, group], s1_ss.at[b, step])
            left_here(sr2.at[b, z], s2_ss.at[b, step])
            left_here(hb.at[y, c, pl.ds(first // 2, count // 2)], hy_ss.at[b, step])
        for side in (0, 1):
            left_here(grads.at[x, pl.ds(first, count // 2)], f_ss.at[b, side])
            for turn in (0, 1):
                left_here(grads.at[x, pl.ds(first, count // 2)], g_ss.at[b, side, turn])
    for zz in range(8):

        @pl.when(zz != z)
        def _():
            left_here(zs.at[zz], hz_ss.at[zz])


PIECES = tuple((lo, min(lo + 256, COLS)) for lo in range(0, COLS, 256))


def hand_on(*refs):
    sources, targets, here, sems = refs[:5], refs[5:10], refs[10:15], refs[15]
    first, second = [], []
    for k, (source, target, stage) in enumerate(zip(sources, targets, here)):
        for lo, hi in PIECES if k == 3 else ((0, source.shape[0]),):
            i = len(first)
            first.append(pltpu.make_async_copy(source.at[lo:hi], stage.at[lo:hi], sems.at[0, i]))
            second.append(pltpu.make_async_copy(stage.at[lo:hi], target.at[lo:hi], sems.at[1, i]))
    for copy in first:
        copy.start()
    for one, two in zip(first, second):
        one.wait()
        two.start()
    for copy in second:
        copy.wait()


def body(teacher_hidden, student_hidden, teacher_weight, student_weight, sampled_ids):
    dma, vmem = pltpu.SemaphoreType.DMA, pltpu.VMEM
    on_chip = pl.BlockSpec(memory_space=pltpu.VMEM)
    any_space = pl.BlockSpec(memory_space=pl.ANY)
    kt, ks = teacher_weight.shape[0], student_weight.shape[0]
    outs = (
        jax.ShapeDtypeStruct((1, 128), F32),
        jax.ShapeDtypeStruct((2, 128), F32),
        jax.ShapeDtypeStruct((COLS, 128), BF16),
        jax.ShapeDtypeStruct((COLS, ks), BF16),
        jax.ShapeDtypeStruct((8, ks), BF16),
    )
    results = pl.pallas_call(
        kernel,
        out_shape=outs,
        in_specs=[any_space] * 5,
        out_specs=(on_chip, on_chip, any_space, any_space, on_chip),
        scratch_shapes=[
            vmem((COLS, kt), BF16), vmem((COLS, ks), BF16),
            vmem((4, 8, 2, 8, kt), BF16), vmem((4, 8, 2, 8, ks), BF16),
            vmem((4, OWN, kt), BF16), vmem((4, OWN, ks), BF16),
            vmem((3, OWN, WIDE), F32), vmem((2, OWN, WIDE), F32),
            vmem((2, OWN, WIDE), I16), vmem((2, 2, OWN // 2, WIDE), I16),
            vmem((2, 2, OWN, WIDE), I16), vmem((2, 2, OWN, WIDE), I16),
            vmem((2, OWN, WIDE), F32),
            vmem((128, 128), F32), vmem((128, 128), F32),
            vmem((3, 8, 8, 128), F32), vmem((3, 8, 8, 128), F32),
            vmem((128, 128), F32), vmem((128, 128), F32), vmem((3, 8, 128), F32),
            vmem((4, OWN, WIDE), BF16),
            vmem((WIDE, ks), F32), vmem((WIDE, ks), BF16), vmem((WIDE, 128), BF16),
            vmem((4, 2, OWN // 2, ks), BF16), vmem((8, OWN // 2, ks), BF16),
            vmem((8, 8, ks), BF16), vmem((8, 8, ks), BF16), vmem((1, 128), jnp.int32),
            dma((5,)), dma((2, 8)), dma((2, 8)), dma((2, 3, 4)), dma((2, 3, 4)), dma((2, 3)), dma((2, 3)),
            dma((2, 3, 2)), dma((2, 3, 2)), dma((2, 3, 2)), dma((2, 3, 2)),
            dma((3, 8)), dma((3, 8)), dma((3, 8)), dma((3, 8)),
            dma((3, 2, 2)), dma((3, 2, 2)), dma((3, 2)), dma((3, 2)),
            dma((3, 8)), dma((3, 8)), dma((8,)), dma((8,)), dma((2,)),
        ],
        compiler_params=pltpu.CompilerParams(
            collective_id=0, has_side_effects=True, vmem_limit_bytes=60 * 1024 * 1024
        ),
    )(teacher_hidden, student_hidden, sampled_ids.reshape(1, 128), teacher_weight.T, student_weight.T)
    kl, chosen, grad, weight_grad, hidden_grad = pl.pallas_call(
        hand_on,
        out_shape=outs,
        in_specs=[any_space] * 5,
        out_specs=[any_space] * 5,
        scratch_shapes=[vmem(out.shape, out.dtype) for out in outs] + [dma((2, len(PIECES) + 4))],
        compiler_params=pltpu.CompilerParams(vmem_limit_bytes=60 * 1024 * 1024),
    )(*results)
    return kl.reshape(128), chosen, grad.T, weight_grad.T, hidden_grad


def solution(mesh):
    placed = (P("vocab", "row"), P("vocab", "row"), P("row", "vocab"), P("row", "vocab"), P("row"))
    return jax.shard_map(
        body,
        mesh=mesh,
        in_specs=placed,
        out_specs=(P("row"), P(None, "row"), P("row", "vocab"), P("row", "vocab"), P("vocab", "row")),
        check_vma=False,
    )
```

```python
import jax
import jax.numpy as jnp
from jax import lax
from jax.experimental import pallas as pl
from jax.experimental.pallas import tpu as pltpu
from jax.sharding import PartitionSpec as P

MESH = pl.DeviceIdType.MESH
F32, BF16, I16 = jnp.float32, jnp.bfloat16, jnp.int16
NX, NY, NZ, NC = 4, 4, 8, 2
OWN = 128
PARTS = ((0, 64), (64, 32), (96, 32))
COLS = 2000
WIDE = 2048
TAIL = WIDE - 128
GROUP = 16
FAR_FIRST = (4, 3, 5, 2, 6, 1, 7)
BESIDE = (5, 4, 2, 3, 6, 7, 1)
SCALE = 32000.0
BLOCKS = ((0, 512), (512, 1024), (1024, 1536), (1536, COLS))


def softcap(values):
    return 30.0 * jnp.tanh(values * (1.0 / 30.0))


def encode(values, ref, at):
    most = jnp.max(jnp.abs(values), axis=1, keepdims=True)
    power = jnp.ceil(jnp.log2(jnp.maximum(most, 1e-30)))
    whole = jnp.round(values * (jnp.exp2(-power) * SCALE))
    lane = lax.broadcasted_iota(jnp.int32, (values.shape[0], 128), 1)
    last = jnp.where(lane >= COLS - TAIL, power, whole[:, TAIL:])
    ref[at, 0:TAIL] = whole[:, :TAIL].astype(I16)
    ref[at, TAIL:WIDE] = last.astype(I16)


def decode(ref, at):
    values = ref[at, :].astype(F32)
    lane = lax.broadcasted_iota(jnp.int32, (values.shape[0], 128), 1)
    power = jnp.max(jnp.where(lane >= COLS - TAIL, values[:, TAIL:], -1000.0), axis=1, keepdims=True)
    return values * (jnp.exp2(power) * (1.0 / SCALE))


def kernel(
    th, sh, ids, wt_hbm, ws_hbm,
    kl_out, chosen_out, grad_out, wg_out, hg_out,
    wt, ws, ht, hs, lt, ls, part, own_part, one_s, one_r, two_s, two_r, logits, stat, ids_at, sr1, sr2, res, res_at, back,
    grads, wg_acc, wg_stage, grad_stage, hb, yr, zs, zr,
    ids_here, w_sem, zsnd, zrcv, ysnd, yrcv, csnd, crcv,
    one_ss, one_rs, two_ss, two_rs, s1_ss, s1_rs, s2_ss, s2_rs, g_ss, g_rs, f_ss, f_rs,
    hy_ss, hy_rs, hz_ss, hz_rs, out_sem,
):
    x = lax.axis_index("row")
    v = lax.axis_index("vocab")
    y, z, c = v // 16, (v // 2) % 8, v % 2
    right, left, across = (x + 1) % 4, (x + 3) % 4, (x + 2) % 4

    def at_x(to):
        return (to, v)

    def at_v(ty, tz, tc):
        return (x, ty * 16 + tz * 2 + tc)

    def remote(src, dst, ss, rs, device):
        return pltpu.make_async_remote_copy(
            src_ref=src, dst_ref=dst, send_sem=ss, recv_sem=rs, device_id=device, device_id_type=MESH
        )

    def landed(ref, sem):
        remote(ref, ref, sem, sem, at_x(right)).wait_recv()

    def left_here(ref, sem):
        remote(ref, ref, sem, sem, at_x(right)).wait_send()

    barrier = pltpu.get_barrier_semaphore()
    for to in (right, left):
        pl.semaphore_signal(barrier, inc=1, device_id=at_x(to), device_id_type=MESH)
    for step in FAR_FIRST:
        pl.semaphore_signal(
            barrier, inc=1, device_id=at_v((y + step // 2) % 4, z, (c + step) % 2), device_id_type=MESH
        )
        pl.semaphore_signal(barrier, inc=1, device_id=at_v(y, (z + step) % 8, c), device_id_type=MESH)

    loads = [
        pltpu.make_async_copy(source, target, w_sem.at[i])
        for i, (source, target) in enumerate(
            ((sh, hs.at[y, z, c]), (th, ht.at[y, z, c]), (ids, ids_here), (ws_hbm, ws), (wt_hbm, wt))
        )
    ]
    for load in loads:
        load.start()
    part[:, :, TAIL:WIDE] = jnp.zeros((3, OWN, 128), F32)
    own_part[:, :, TAIL:WIDE] = jnp.zeros((2, OWN, 128), F32)
    stat[...] = jnp.zeros((128, 128), F32)
    res[...] = jnp.zeros((128, 128), F32)
    for load in loads[:3]:
        load.wait()
    ids_at[...] = jnp.transpose(jnp.broadcast_to(ids_here[...].astype(F32), (128, 128)))

    pl.semaphore_wait(barrier, 16)

    both = ((0, hs), (1, ht))
    def z_send(m, ref):
        for step in FAR_FIRST:
            to = (z + step) % 8
            remote(
                ref.at[y, z, c], ref.at[y, z, c], zsnd.at[m, step], zrcv.at[m, z], at_v(y, to, c)
            ).start()

    z_send(0, hs)

    def block_rows(b):
        first, rows = PARTS[b]
        return first // 16, rows // 16

    def z_arrive(m, ref, b):
        first, count = block_rows(b)
        for zz in range(first, first + count):

            @pl.when(zz != z)
            def _():
                landed(ref.at[y, zz, c], zrcv.at[m, zz])

    def y_send(m, ref, b):
        src = ref.at[y, pl.ds(*block_rows(b)), c]
        for step in (2, 1, 3):
            remote(
                src, src, ysnd.at[m, b, step], yrcv.at[m, b, y], at_v((y + step) % 4, z, c)
            ).start()

    def y_arrive(m, ref, b):
        for step in (2, 1, 3):
            yy = (y + step) % 4
            landed(ref.at[yy, pl.ds(*block_rows(b)), c], yrcv.at[m, b, yy])

    def c_send(m, ref, b):
        src = ref.at[:, pl.ds(*block_rows(b)), c]
        remote(src, src, csnd.at[m, b], crcv.at[m, b], at_v(y, z, 1 - c)).start()

    def c_arrive(m, ref, b):
        first, count = block_rows(b)
        landed(ref.at[:, pl.ds(first, count), 1 - c], crcv.at[m, b])
        rows = (ls, lt)[m]
        for k in range(4):
            block = ref[k, first : first + count].astype(F32)
            rows[k, 16 * first : 16 * (first + count), :] = block.reshape(16 * count, rows.shape[-1]).astype(BF16)

    def product(m, b, chunks, targets):
        first, count = PARTS[b]
        rows, weight = (ls, ws) if m == 0 else (lt, wt)
        lhs = jnp.concatenate([rows[chunk, first : first + count, :] for chunk in chunks], axis=0)
        for lo, hi in BLOCKS:
            block = lax.dot_general(
                lhs, weight[lo:hi, :], (((1,), (1,)), ((), ())), preferred_element_type=F32
            )
            for i, target in enumerate(targets):
                target[first : first + count, lo:hi] = block[i * count : (i + 1) * count, :]

    def hop_one(m, b):
        first, count = PARTS[b]
        product(m, b, (across, x), (part.at[0], own_part.at[m]))

        @pl.loop(0, count // GROUP)
        def _(g):
            at = pl.ds(pl.multiple_of(first + g * GROUP, GROUP), GROUP)
            encode(part[0, at, :], one_s.at[m], at)

        some = count // 2
        for side, to in ((0, right), (1, left)):
            remote(
                one_s.at[m, pl.ds(first + side * some, some)], one_r.at[m, side, pl.ds(first // 2, some)],
                one_ss.at[m, b, side], one_rs.at[m, b, side], at_x(to),
            ).start()

    def hop_two(m, b):
        first, count = PARTS[b]
        some = count // 2
        product(m, b, (right, left), (part.at[1], part.at[2]))
        for side, to in ((0, right), (1, left)):
            landed(one_r.at[m, side, pl.ds(first // 2, some)], one_rs.at[m, b, side])

            @pl.loop(0, some // GROUP)
            def _(g):
                inner = pl.ds(pl.multiple_of(first // 2 + g * GROUP, GROUP), GROUP)
                at = pl.ds(pl.multiple_of(first + side * some + g * GROUP, GROUP), GROUP)
                plain = pl.ds(pl.multiple_of(first + (1 - side) * some + g * GROUP, GROUP), GROUP)
                encode(part[1 + side, at, :] + decode(one_r.at[m, side], inner), two_s.at[m, side], at)
                encode(part[1 + side, plain, :], two_s.at[m, side], plain)

            at = pl.ds(first, count)
            remote(
                two_s.at[m, side, at], two_r.at[m, side, at], two_ss.at[m, b, side], two_rs.at[m, b, side], at_x(to)
            ).start()

    def finish(m, b):
        first, count = PARTS[b]
        for side in (0, 1):
            landed(two_r.at[m, side, pl.ds(first, count)], two_rs.at[m, b, side])
        column = lax.broadcasted_iota(jnp.int32, (GROUP, WIDE), 1)
        lane = lax.broadcasted_iota(jnp.int32, (GROUP, 128), 1)

        @pl.loop(0, count // GROUP)
        def _(g):
            at = pl.ds(pl.multiple_of(first + g * GROUP, GROUP), GROUP)
            raw = own_part[m, at, :] + decode(two_r.at[m, 0], at) + decode(two_r.at[m, 1], at)
            capped = softcap(raw)
            logits[m, at, :] = capped
            if m == 1:
                student = logits[0, at, :]
                valid = column < COLS
                t_exp = jnp.where(valid, jnp.exp(capped), 0.0)
                s_exp = jnp.where(valid, jnp.exp(student), 0.0)
                wanted = ids_at[at, 0:1].astype(jnp.int32) - v * COLS
                hit = jnp.logical_and(column == wanted, valid)
                sums = (
                    t_exp,
                    jnp.where(hit, capped, 0.0),
                    s_exp,
                    s_exp * (student - capped),
                    jnp.where(hit, student, 0.0),
                )
                tile = jnp.zeros((GROUP, 128), F32)
                for j, term in enumerate(sums):
                    tile = jnp.where(lane == j, jnp.sum(term, axis=1, keepdims=True), tile)
                stat[at, :] = tile

    group = y * 2 + c

    def stats_one(half):
        sr1[half, group] = jnp.transpose(stat[...])[0:8, :]
        for step in BESIDE:
            remote(
                sr1.at[half, group], sr1.at[half, group], s1_ss.at[half, step], s1_rs.at[half, group],
                at_v((y + step // 2) % 4, z, (c + step) % 2),
            ).start()

    def stats_two(half):
        for step in range(1, 8):
            who = ((y + step // 2) % 4) * 2 + (c + step) % 2
            landed(sr1.at[half, who], s1_rs.at[half, who])
        total = sr1[half, 0]
        for k in range(1, 8):
            total = total + sr1[half, k]
        sr2[half, z] = total
        for step in FAR_FIRST:
            remote(
                sr2.at[half, z], sr2.at[half, z], s2_ss.at[half, step], s2_rs.at[half, z],
                at_v(y, (z + step) % 8, c),
            ).start()

    def gradient(half):
        for step in range(1, 8):
            who = (z + step) % 8
            landed(sr2.at[half, who], s2_rs.at[half, who])
        total = sr2[half, 0]
        for k in range(1, 8):
            total = total + sr2[half, k]
        t_total, t_pick, s_total, cross, s_pick = (total[j : j + 1, :] for j in range(5))
        s_log, t_log = jnp.log(s_total), jnp.log(t_total)
        divergence = cross / s_total - s_log + t_log
        res[0:1, :] = 1.0 / s_total
        res[1:2, :] = t_log - s_log - divergence
        back[half, 0:1, :] = divergence
        back[half, 1:2, :] = s_pick - s_log
        back[half, 2:3, :] = t_pick - t_log
        res_at[...] = jnp.transpose(res[...])

        first, count = PARTS[half]

        @pl.loop(0, count // GROUP)
        def _(g):
            at = pl.ds(pl.multiple_of(first + g * GROUP, GROUP), GROUP)
            student, teacher = logits[0, at, :], logits[1, at, :]
            inverse, shift = res_at[at, 0:1], res_at[at, 1:2]
            ratio = student * (1.0 / 30.0)
            grads[x, at, :] = (
                jnp.exp(student) * inverse * (student - teacher + shift) * (1.0 - ratio * ratio)
            ).astype(BF16)

        some = count // 2
        for turn in (0, 1):
            for side, to in ((0, right), (1, left)):
                mine = grads.at[x, pl.ds(first + some * ((side + turn) % 2), some)]
                remote(mine, mine, g_ss.at[half, side, turn], g_rs.at[half, side, turn], at_x(to)).start()

    def forward(b):
        first, count = PARTS[b]
        some = count // 2
        for side, chunk, to in ((0, left, right), (1, right, left)):
            src = grads.at[chunk, pl.ds(first + some * side, some)]
            landed(src, g_rs.at[b, side, 0])
            remote(src, src, f_ss.at[b, side], f_rs.at[b, side], at_x(to)).start()

    def gathered(b):
        first, count = PARTS[b]
        some = count // 2
        landed(grads.at[left, pl.ds(first + some, some)], g_rs.at[b, 0, 1])
        landed(grads.at[right, pl.ds(first, some)], g_rs.at[b, 1, 1])
        landed(grads.at[across, pl.ds(first, some)], f_rs.at[b, 0])
        landed(grads.at[across, pl.ds(first + some, some)], f_rs.at[b, 1])

    def hidden_product(b):
        first, count = PARTS[b]
        rows = grads[:, first : first + count, 0:COLS].reshape(NX * count, COLS)
        at = slice(first // 2, (first + count) // 2)
        for lo, hi in ((0, 256), (256, 512), (512, 768), (768, 896)):
            block = jnp.dot(rows, ws[:, lo:hi], preferred_element_type=F32)
            block = block.reshape(4, count // 16, 2, 8, hi - lo)
            for k in range(4):
                for core in range(2):
                    hb[k, core, at, lo:hi] = block[k, :, core].reshape(count // 2, hi - lo).astype(BF16)
        at = pl.ds(first // 2, count // 2)
        for step in BESIDE:
            ty, tc = (y + step // 2) % 4, (c + step) % 2
            remote(
                hb.at[ty, tc, at], yr.at[group, at], hy_ss.at[b, step], hy_rs.at[b, group], at_v(ty, z, tc)
            ).start()

    def weight_product(half):
        rows = ls[:, half * 64 : half * 64 + 64, :].reshape(NX * 64, ls.shape[-1])

        @pl.loop(0, WIDE // 256)
        def _(i):
            at = pl.ds(pl.multiple_of(i * 256, 256), 256)
            lhs = grads[:, half * 64 : half * 64 + 64, at].reshape(NX * 64, 256)
            block = lax.dot_general(lhs, rows, (((0,), (0,)), ((), ())), preferred_element_type=F32)
            if half == 0:
                wg_acc[at, :] = block
            else:
                wg_stage[at, :] = (wg_acc[at, :] + block).astype(BF16)

    def own_gradient():
        @pl.loop(0, WIDE // 128)
        def _(i):
            at = pl.ds(pl.multiple_of(i * 128, 128), 128)
            grad_stage[at, :] = jnp.transpose(grads[x, :, at].astype(F32)).astype(BF16)

    def hidden_z(b):
        first, count = block_rows(b)
        at = pl.ds(8 * first, 8 * count)
        total = hb[y, c, 8 * first : 8 * (first + count), :].astype(F32)
        for step in range(1, 8):
            who = ((y + step // 2) % 4) * 2 + (c + step) % 2
            landed(yr.at[who, at], hy_rs.at[b, who])
            total = total + yr[who, 8 * first : 8 * (first + count), :].astype(F32)
        zs[first : first + count] = total.reshape(count, 8, 896).astype(BF16)
        for zz in range(first, first + count):

            @pl.when(zz != z)
            def _():
                remote(zs.at[zz], zr.at[z], hz_ss.at[zz], hz_rs.at[z], at_v(y, zz, c)).start()

    def hidden_end():
        zr[z] = zs[z]
        for step in range(1, 8):
            who = (z + step) % 8
            landed(zr.at[who], hz_rs.at[who])
        total = zr[0].astype(F32)
        for k in range(1, 8):
            total = total + zr[k].astype(F32)
        hg_out[...] = total.astype(BF16)

    S, T = 0, 1
    z_arrive(S, hs, 0)
    y_send(S, hs, 0)
    z_send(T, ht)
    for b in (1, 2):
        z_arrive(S, hs, b)
        y_send(S, hs, b)
    y_arrive(S, hs, 0)
    c_send(S, hs, 0)
    for b in range(3):
        z_arrive(T, ht, b)
        y_send(T, ht, b)
    c_arrive(S, hs, 0)
    loads[3].wait()
    hop_one(S, 0)
    for b in (1, 2):
        y_arrive(S, hs, b)
        c_send(S, hs, b)
    for b in (1, 2):
        c_arrive(S, hs, b)
        hop_one(S, b)
    y_arrive(T, ht, 0)
    c_send(T, ht, 0)
    hop_two(S, 0)
    loads[4].wait()
    c_arrive(T, ht, 0)
    hop_one(T, 0)
    for b in (1, 2):
        y_arrive(T, ht, b)
        c_send(T, ht, b)
    hop_two(S, 1)
    hop_two(T, 0)
    for b in (1, 2):
        c_arrive(T, ht, b)
        hop_one(T, b)
    finish(S, 0)
    hop_two(S, 2)
    finish(T, 0)
    stats_one(0)
    hop_two(T, 1)
    hop_two(T, 2)
    finish(S, 1)
    stats_two(0)
    finish(T, 1)
    stats_one(1)
    finish(S, 2)
    gradient(0)
    stats_two(1)
    finish(T, 2)
    stats_one(2)
    forward(0)
    gradient(1)
    stats_two(2)
    forward(1)
    gradient(2)
    gathered(0)
    hidden_product(0)
    forward(2)
    gathered(1)
    hidden_product(1)
    own_gradient()
    store_grad = pltpu.make_async_copy(grad_stage.at[pl.ds(0, COLS)], grad_out, out_sem.at[1])
    store_grad.start()
    hidden_z(0)
    weight_product(0)
    gathered(2)
    hidden_product(2)
    hidden_z(1)
    weight_product(1)
    store = pltpu.make_async_copy(wg_stage.at[pl.ds(0, COLS)], wg_out, out_sem.at[0])
    store.start()
    hidden_z(2)
    lane = lax.broadcasted_iota(jnp.int32, (1, 128), 1)
    final = back[0]
    for b in (1, 2):
        final = jnp.where(lane < PARTS[b][0], final, back[b])
    kl_out[...] = final[0:1, :]
    chosen_out[...] = final[1:3, :]
    hidden_end()
    store.wait()
    store_grad.wait()

    for m, ref in both:
        for step in range(1, 8):
            left_here(ref.at[y, z, c], zsnd.at[m, step])
        for b in range(3):
            for step in (1, 2, 3):
                left_here(ref.at[y, pl.ds(*block_rows(b)), c], ysnd.at[m, b, step])
            left_here(ref.at[:, pl.ds(*block_rows(b)), c], csnd.at[m, b])
    for m in (0, 1):
        for b, (first, count) in enumerate(PARTS):
            for side in (0, 1):
                left_here(one_s.at[m, pl.ds(first, count // 2)], one_ss.at[m, b, side])
                left_here(two_s.at[m, side, pl.ds(first, count)], two_ss.at[m, b, side])
    for b, (first, count) in enumerate(PARTS):
        for step in range(1, 8):
            left_here(sr1.at[b, group], s1_ss.at[b, step])
            left_here(sr2.at[b, z], s2_ss.at[b, step])
            left_here(hb.at[y, c, pl.ds(first // 2, count // 2)], hy_ss.at[b, step])
        for side in (0, 1):
            left_here(grads.at[x, pl.ds(first, count // 2)], f_ss.at[b, side])
            for turn in (0, 1):
                left_here(grads.at[x, pl.ds(first, count // 2)], g_ss.at[b, side, turn])
    for zz in range(8):

        @pl.when(zz != z)
        def _():
            left_here(zs.at[zz], hz_ss.at[zz])


PIECES = tuple((lo, min(lo + 256, COLS)) for lo in range(0, COLS, 256))


def hand_on(*refs):
    sources, targets, here, sems = refs[:5], refs[5:10], refs[10:15], refs[15]
    first, second = [], []
    for k, (source, target, stage) in enumerate(zip(sources, targets, here)):
        for lo, hi in PIECES if k == 3 else ((0, source.shape[0]),):
            i = len(first)
            first.append(pltpu.make_async_copy(source.at[lo:hi], stage.at[lo:hi], sems.at[0, i]))
            second.append(pltpu.make_async_copy(stage.at[lo:hi], target.at[lo:hi], sems.at[1, i]))
    for copy in first:
        copy.start()
    for one, two in zip(first, second):
        one.wait()
        two.start()
    for copy in second:
        copy.wait()


def body(teacher_hidden, student_hidden, teacher_weight, student_weight, sampled_ids):
    dma, vmem = pltpu.SemaphoreType.DMA, pltpu.VMEM
    on_chip = pl.BlockSpec(memory_space=pltpu.VMEM)
    any_space = pl.BlockSpec(memory_space=pl.ANY)
    kt, ks = teacher_weight.shape[0], student_weight.shape[0]
    outs = (
        jax.ShapeDtypeStruct((1, 128), F32),
        jax.ShapeDtypeStruct((2, 128), F32),
        jax.ShapeDtypeStruct((COLS, 128), BF16),
        jax.ShapeDtypeStruct((COLS, ks), BF16),
        jax.ShapeDtypeStruct((8, ks), BF16),
    )
    results = pl.pallas_call(
        kernel,
        out_shape=outs,
        in_specs=[any_space] * 5,
        out_specs=(on_chip, on_chip, any_space, any_space, on_chip),
        scratch_shapes=[
            vmem((COLS, kt), BF16), vmem((COLS, ks), BF16),
            vmem((4, 8, 2, 8, kt), BF16), vmem((4, 8, 2, 8, ks), BF16),
            vmem((4, OWN, kt), BF16), vmem((4, OWN, ks), BF16),
            vmem((3, OWN, WIDE), F32), vmem((2, OWN, WIDE), F32),
            vmem((2, OWN, WIDE), I16), vmem((2, 2, OWN // 2, WIDE), I16),
            vmem((2, 2, OWN, WIDE), I16), vmem((2, 2, OWN, WIDE), I16),
            vmem((2, OWN, WIDE), F32),
            vmem((128, 128), F32), vmem((128, 128), F32),
            vmem((3, 8, 8, 128), F32), vmem((3, 8, 8, 128), F32),
            vmem((128, 128), F32), vmem((128, 128), F32), vmem((3, 8, 128), F32),
            vmem((4, OWN, WIDE), BF16),
            vmem((WIDE, ks), F32), vmem((WIDE, ks), BF16), vmem((WIDE, 128), BF16),
            vmem((4, 2, OWN // 2, ks), BF16), vmem((8, OWN // 2, ks), BF16),
            vmem((8, 8, ks), BF16), vmem((8, 8, ks), BF16), vmem((1, 128), jnp.int32),
            dma((5,)), dma((2, 8)), dma((2, 8)), dma((2, 3, 4)), dma((2, 3, 4)), dma((2, 3)), dma((2, 3)),
            dma((2, 3, 2)), dma((2, 3, 2)), dma((2, 3, 2)), dma((2, 3, 2)),
            dma((3, 8)), dma((3, 8)), dma((3, 8)), dma((3, 8)),
            dma((3, 2, 2)), dma((3, 2, 2)), dma((3, 2)), dma((3, 2)),
            dma((3, 8)), dma((3, 8)), dma((8,)), dma((8,)), dma((2,)),
        ],
        compiler_params=pltpu.CompilerParams(
            collective_id=0, has_side_effects=True, vmem_limit_bytes=60 * 1024 * 1024
        ),
    )(teacher_hidden, student_hidden, sampled_ids.reshape(1, 128), teacher_weight.T, student_weight.T)
    kl, chosen, grad, weight_grad, hidden_grad = pl.pallas_call(
        hand_on,
        out_shape=outs,
        in_specs=[any_space] * 5,
        out_specs=[any_space] * 5,
        scratch_shapes=[vmem(out.shape, out.dtype) for out in outs] + [dma((2, len(PIECES) + 4))],
        compiler_params=pltpu.CompilerParams(vmem_limit_bytes=60 * 1024 * 1024),
    )(*results)
    return kl.reshape(128), chosen, grad.T, weight_grad.T, hidden_grad


def solution(mesh):
    placed = (P("vocab", "row"), P("vocab", "row"), P("row", "vocab"), P("row", "vocab"), P("row"))
    return jax.shard_map(
        body,
        mesh=mesh,
        in_specs=placed,
        out_specs=(P("row"), P(None, "row"), P("row", "vocab"), P("row", "vocab"), P("vocab", "row")),
        check_vma=False,
    )
```
